128 devices in a mesh: src: 8 (over x, y_lo), tgt: 16 (over y_hi, z, core).
Axes of the slice: x: 4, y: 4 (y_hi: 2, y_lo: 2; y = y_hi * 2 + y_lo), z: 4, core: 2. Of those that a mesh axis runs over, the one named last changes fastest.
Arguments:
- source_weights: bfloat16 [16, 16, 1024, 128], P('src', 'tgt'), may hold values from -6 to 6
- wave_speed: float32 [2, 3], replicated, may hold values from 0.25 to 1
- offsets: float32 [32, 4], replicated, may hold values from 1 to 2
Outputs:
- target_weights: float32 [16, 16, 1024, 128], P(None, None, ('src', 'tgt'))
The draws below stay inside these ranges and needn't reach their ends.
All inputs are finite; a program needn't handle non-finite values.
Results may differ from the reference program's by a relative error of at most 0.0003.
Values sent between devices are 32-bit elements; how exact they have to be, the bound alone decides.
A program may use at most 64 MiB of HBM per device.

```python
import math
import jax
import jax.numpy as jnp
from jax import lax

POINTS = 8
BOXES = 16
R = 32
OUTERS = 32
COLS = 1024


def block_levels(stream_key, shape, pieces, least, largest):
    def one(axis_at, parts):
        draws = jax.random.uniform(jax.random.fold_in(jax.random.fold_in(stream_key, 6), axis_at), (parts,), jnp.float32, least / len(pieces), largest / len(pieces))
        return jnp.repeat(jnp.exp(draws), shape[axis_at] // parts).reshape((-1,) + (1,) * (len(shape) - axis_at - 1))

    loudness = one(*pieces[0])
    for cut in pieces[1:]:
        loudness = loudness * one(*cut)
    return loudness


def centred(stream_key, extent, scale, bound, cuts=(), kind=jnp.bfloat16):
    array = scale * jax.random.normal(stream_key, extent, jnp.float32)
    if cuts:
        array = array * block_levels(stream_key, extent, cuts, -0.22, 0.18)
    return jnp.clip(array, -bound, bound).astype(kind)


def setup_inputs(seed: int = 0) -> dict:
    keys = jax.random.split(jax.random.key(seed), 4)
    source_weights = centred(keys[0], (BOXES, BOXES, COLS, 2 * POINTS * POINTS), 1.0, 6.0, ((0, 8), (1, 16)))
    wave_speed = jnp.clip(jax.random.uniform(keys[1], (2, 3), jnp.float32, 0.25, 1.0), 0.25, 1.0)
    offsets = jnp.clip(jax.random.uniform(keys[2], (OUTERS, 4), jnp.float32, 1.0, 2.0), 1.0, 2.0)
    return dict(source_weights=source_weights, wave_speed=wave_speed, offsets=offsets)


PHASE_SCALE = 4096.0

def chebyshev_nodes():
    counter = jnp.arange(8, dtype=jnp.float32)
    return 0.5 - 0.5 * jnp.cos((2.0 * counter + 1.0) * (math.pi / 16.0))

def layout_tables(merge_axis):
    node_values = chebyshev_nodes()
    column = jnp.arange(128, dtype=jnp.int32)
    child_side = column // 64
    first_axis = column // 8 % 8
    second_axis = column % 8
    parent_point = jnp.arange(64, dtype=jnp.int32)
    parent_first = parent_point // 8
    parent_second = parent_point % 8
    if merge_axis == 0:
        merge_col, other_col, merge_pt, other_pt = (first_axis, second_axis, parent_first, parent_second)
    else:
        merge_col, other_col, merge_pt, other_pt = (second_axis, first_axis, parent_second, parent_first)
    child_merge = child_side.astype(jnp.float32) + node_values[merge_col]
    child_other = node_values[other_col]
    parent_merge = node_values[merge_pt]
    parent_other = node_values[other_pt]
    spread = child_merge[:, None] / 2.0 - node_values[None, :]
    node_gaps = node_values[:, None] - node_values[None, :]
    diagonal = jnp.eye(8, dtype=bool)
    factors = jnp.where(diagonal[None], 1.0, spread[:, None, :] / jnp.where(diagonal, 1.0, node_gaps)[None])
    lagrange = jnp.prod(factors, axis=2)
    basis_table = lagrange[:, merge_pt] * (other_col[:, None] == other_pt[None, :]).astype(jnp.float32)
    return (child_merge, child_other, parent_merge, parent_other, basis_table)

def bit_value(number, bit_place):
    return number // 2 ** bit_place % 2

def source_position(number, done_count):
    accumulated = jnp.zeros_like(number)
    for position_bit in range(done_count, 4):
        accumulated = accumulated + bit_value(number, 3 - position_bit) * 2 ** (position_bit - done_count)
    return accumulated

def speeds(wave_speed, first_coord, second_coord):
    first_speed = wave_speed[0, 0] + wave_speed[0, 1] * first_coord + wave_speed[0, 2] * second_coord
    second_speed = wave_speed[1, 0] + wave_speed[1, 1] * first_coord + wave_speed[1, 2] * second_coord
    return (first_speed, second_speed)

def phase_angle(target_merge, target_other, speed_merge, speed_other, refer_merge, refer_other, delta_merge, delta_other):
    point_merge = refer_merge + delta_merge
    point_other = refer_other + delta_other
    square_merge = speed_merge * speed_merge
    square_other = speed_other * speed_other
    numerator = square_merge * delta_merge * (point_merge + refer_merge) + square_other * delta_other * (point_other + refer_other)
    denominator = jnp.sqrt(square_merge * point_merge * point_merge + square_other * point_other * point_other) + jnp.sqrt(square_merge * refer_merge * refer_merge + square_other * refer_other * refer_other)
    return PHASE_SCALE * (target_merge * delta_merge + target_other * delta_other + numerator / denominator)

def advance(lower_box, upper_box, child_bit, merge_index, other_index, offsets, wave_speed, merge_axis, done_merge, done_other):
    child_merge, child_other, parent_merge, parent_other, basis_table = layout_tables(merge_axis)
    if merge_axis == 0:
        anchor_merge, anchor_other, source_merge, source_other = (offsets[:, 0], offsets[:, 1], offsets[:, 2], offsets[:, 3])
    else:
        anchor_merge, anchor_other, source_merge, source_other = (offsets[:, 1], offsets[:, 0], offsets[:, 3], offsets[:, 2])
    target_split = merge_index // 2 ** (4 - done_merge)
    source_parent = source_position(merge_index, done_merge) // 2
    target_fixed = other_index // 2 ** (4 - done_other)
    source_fixed = source_position(other_index, done_other)
    width_merge = 2.0 ** (-2 - done_merge)
    width_other = 2.0 ** (-2 - done_other)
    cell_merge = 2.0 ** (done_merge - 10)
    cell_other = 2.0 ** (done_other - 10)
    target_merge = anchor_merge + (2.0 * target_split.astype(jnp.float32) + child_bit.astype(jnp.float32) + 0.5) * (width_merge / 2.0)
    target_other = anchor_other + (target_fixed.astype(jnp.float32) + 0.5) * width_other
    refer_merge = source_merge + source_parent.astype(jnp.float32) * (2.0 * cell_merge)
    refer_other = source_other + source_fixed.astype(jnp.float32) * cell_other
    if merge_axis == 0:
        first_speed, second_speed = speeds(wave_speed, target_merge, target_other)
        speed_merge, speed_other = (first_speed, second_speed)
    else:
        first_speed, second_speed = speeds(wave_speed, target_other, target_merge)
        speed_merge, speed_other = (second_speed, first_speed)

    def widen(array_in):
        return array_in[..., None]
    angle_in = phase_angle(widen(target_merge), widen(target_other), widen(speed_merge), widen(speed_other), widen(refer_merge), widen(refer_other), cell_merge * child_merge, cell_other * child_other)
    angle_out = phase_angle(widen(target_merge), widen(target_other), widen(speed_merge), widen(speed_other), widen(refer_merge), widen(refer_other), 2.0 * cell_merge * parent_merge, cell_other * parent_other)
    cos_in = jnp.cos(angle_in)[..., None, :]
    sin_in = jnp.sin(angle_in)[..., None, :]
    cos_out = jnp.cos(angle_out)[..., None, :]
    sin_out = jnp.sin(angle_out)[..., None, :]
    real_in = jnp.concatenate([lower_box[..., :64], upper_box[..., :64]], axis=-1)
    imag_in = jnp.concatenate([lower_box[..., 64:], upper_box[..., 64:]], axis=-1)
    turned = jnp.stack([real_in * cos_in - imag_in * sin_in, real_in * sin_in + imag_in * cos_in])
    projected = jnp.einsum('...s,st->...t', turned, basis_table, precision=lax.Precision.HIGHEST)
    real_out = projected[0] * cos_out + projected[1] * sin_out
    imag_out = projected[1] * cos_out - projected[0] * sin_out
    return jnp.concatenate([real_out, imag_out], axis=-1)

def split_pair(weights_now, axis_pos, bit_place):
    dims_old = weights_now.shape
    group_count = dims_old[axis_pos] // (2 * 2 ** bit_place)
    grouped = weights_now.reshape(dims_old[:axis_pos] + (group_count, 2, 2 ** bit_place) + dims_old[axis_pos + 1:])
    half_dims = dims_old[:axis_pos] + (dims_old[axis_pos] // 2,) + dims_old[axis_pos + 1:]
    lower_part = lax.index_in_dim(grouped, 0, axis_pos + 1, keepdims=False).reshape(half_dims)
    upper_part = lax.index_in_dim(grouped, 1, axis_pos + 1, keepdims=False).reshape(half_dims)
    return (lower_part, upper_part)

def join_pair(first_part, second_part, axis_pos, bit_place, dims_old):
    group_count = dims_old[axis_pos] // (2 * 2 ** bit_place)
    inner_dims = dims_old[:axis_pos] + (group_count, 2 ** bit_place) + dims_old[axis_pos + 1:]
    joined = jnp.stack([first_part.reshape(inner_dims), second_part.reshape(inner_dims)], axis=axis_pos + 1)
    return joined.reshape(dims_old)

def local_level(weights_now, base_first, base_second, offsets, wave_speed, merge_axis, done_merge, done_other):
    bit_place = 3 - done_merge
    lower_part, upper_part = split_pair(weights_now, merge_axis, bit_place)
    if merge_axis == 0:
        merge_base, other_base = (base_first, base_second)
    else:
        merge_base, other_base = (base_second, base_first)
    merge_low = merge_base.reshape(-1, 2, 2 ** bit_place)[:, 0].reshape(-1)
    if merge_axis == 0:
        merge_index = merge_low[:, None, None]
        other_index = other_base[None, :, None]
    else:
        merge_index = merge_low[None, :, None]
        other_index = other_base[:, None, None]
    children = [advance(lower_part, upper_part, jnp.asarray(child_bit, jnp.int32), merge_index, other_index, offsets, wave_speed, merge_axis, done_merge, done_other) for child_bit in (0, 1)]
    return join_pair(children[0], children[1], merge_axis, bit_place, weights_now.shape)

def reference(source_weights, wave_speed, offsets):

    def one_outer(packed):
        weights_block, offset_row = packed
        weights_now = weights_block[:, :, None]
        offset_rows = offset_row[None]
        base_first = jnp.arange(weights_now.shape[0], dtype=jnp.int32)
        base_second = jnp.arange(weights_now.shape[1], dtype=jnp.int32)
        for current in range(8):
            merge_axis = current % 2
            done_first = (current + 1) // 2
            done_second = current // 2
            if merge_axis == 0:
                done_merge, done_other = (done_first, done_second)
            else:
                done_merge, done_other = (done_second, done_first)
            weights_now = local_level(weights_now, base_first, base_second, offset_rows, wave_speed, merge_axis, done_merge, done_other)
        return weights_now[:, :, 0]
    widened = source_weights.astype(jnp.float32)
    dims_old = widened.shape
    grouped = widened.reshape((dims_old[0], dims_old[1], OUTERS, R, dims_old[3]))
    moved = jnp.moveaxis(grouped, 2, 0)
    results = lax.map(one_outer, (moved, offsets))
    return jnp.moveaxis(results, 0, 2).reshape(dims_old)
```

```python
import functools
import math

import jax
import jax.numpy as jnp
import numpy as np
from jax import lax
from jax.experimental import pallas as pl
from jax.experimental.pallas import tpu as pltpu
from jax.sharding import PartitionSpec as P

POINTS = 8
PHASE_SCALE = 4096.0
F32 = jnp.float32
BF16 = jnp.bfloat16


def nodes():
    return 0.5 - 0.5 * np.cos((2.0 * np.arange(8) + 1.0) * (math.pi / 16.0))


def basis(axis):
    z = nodes()
    out = np.zeros((2, 2, 8, 8, 2, 8, 8))
    for s in range(2):
        for p in range(8):
            u = (s + z[p]) / 2.0
            for t in range(8):
                value = 1.0
                for a in range(8):
                    if a != t:
                        value *= (u - z[a]) / (z[t] - z[a])
                for h in range(2):
                    for q in range(8):
                        if axis == 0:
                            out[s, h, p, q, h, t, q] = value
                        else:
                            out[s, h, q, p, h, q, t] = value
    return out.reshape(256, 128)


def basis_split():
    both = []
    for axis in range(2):
        full = basis(axis).astype(np.float32)
        high = full.astype(jnp.bfloat16)
        low = (full - high.astype(np.float32)).astype(jnp.bfloat16)
        both.append(np.concatenate([high, low], axis=1))
    return np.stack(both)


def lane_tables():
    z = nodes().astype(np.float32)
    lane = np.arange(128)
    s, p1, p2 = lane // 64, lane // 8 % 8, lane % 8
    out = np.zeros((8, 4, 128), np.float32)
    for level in range(8):
        k1, k2 = level // 2 + 1, (level + 1) // 2
        w1, w2 = np.float32(2.0 ** (k1 - 10)), np.float32(2.0 ** (k2 - 10))
        if level % 2 == 0:
            out[level, 0] = w1 / 2 * (s.astype(np.float32) + z[p1])
            out[level, 1] = w2 * z[p2]
        else:
            out[level, 0] = w1 * z[p1]
            out[level, 1] = w2 / 2 * (s.astype(np.float32) + z[p2])
        out[level, 2] = w1 * z[p1]
        out[level, 3] = w2 * z[p2]
    return out


def sine_cosine(angle):
    turns = jnp.round(angle * (1.0 / math.pi))
    rest = angle - turns * 3.140625
    rest = rest - turns * 9.67502593994140625e-4
    rest = rest - turns * 1.509957990978376432e-7
    odd = (turns.astype(jnp.int32) & 1) == 1
    sign = jnp.where(odd, -1.0, 1.0)
    sq = rest * rest
    sine = ((2.5997509e-6 * sq - 1.9806479e-4) * sq + 8.3330154e-3) * sq - 1.6666657e-1
    sine = sine * (sq * rest) + rest
    cosine = (2.337661e-5 * sq - 1.3865138e-3) * sq + 4.1665433e-2
    cosine = (cosine * sq - 0.5) * sq + 1.0
    return sine * sign, cosine * sign


def target_index(box, done):
    return box >> (4 - done)


def source_index(box, done):
    total = None
    for place in range(4 - done):
        bit = ((box >> place) & 1) << (3 - done - place)
        total = bit if total is None else total + bit
    return total


def place_of(box, done, target_anchor, source_anchor):
    x = target_anchor + (target_index(box, done).astype(F32) + 0.5) * (2.0 ** (-2 - done))
    source = source_index(box, done)
    if source is None:
        r = source_anchor + jnp.zeros_like(x)
    else:
        r = source_anchor + source.astype(F32) * (2.0 ** (done - 10))
    return x, r


def angle_of(speed, x1, r1, x2, r2, d1, d2):
    s1 = speed[0] + speed[1] * x1 + speed[2] * x2
    s2 = speed[3] + speed[4] * x1 + speed[5] * x2
    a1, a2 = s1 * s1, s2 * s2
    k1, k2 = r1 + d1, r2 + d2
    over = a1 * (d1 * (k1 + r1)) + a2 * (d2 * (k2 + r2))
    under = jnp.sqrt(a1 * (k1 * k1) + a2 * (k2 * k2)) + jnp.sqrt(a1 * (r1 * r1) + a2 * (r2 * r2))
    return PHASE_SCALE * ((x1 * d1 + x2 * d2) + over / under)


def merge_place(level):
    return 3 - level // 2


def make_tables(level, speed, anchor, lanes_ref, cos_ref, sin_ref):
    lane = lax.broadcasted_iota(jnp.int32, (8, 128), 1)
    row = lax.broadcasted_iota(jnp.int32, (8, 128), 0)
    upper = lane >= 64
    side = jnp.where(upper, 1, 0)
    place = merge_place(level)

    def done(which):
        return which // 2 + 1, (which + 1) // 2

    def step(j, carry):
        jv = jnp.zeros((8, 128), jnp.int32) + j
        for half in range(2):
            iv = row + 8 * half
            angle = None
            if level < 8:
                k1, k2 = done(level)
                x1, r1 = place_of(iv, k1, anchor[0], anchor[2])
                x2, r2 = place_of(jv, k2, anchor[1], anchor[3])
                d1, d2 = lanes_ref[level, 0:1, :], lanes_ref[level, 1:2, :]
                angle = angle_of(speed, x1, r1, x2, r2, d1, d2)
            if level > 0:
                k1, k2 = done(level - 1)
                io, jo = iv, jv
                if level < 8 and level % 2 == 0:
                    io = (iv & ~(1 << place)) | (side << place)
                elif level < 8:
                    jo = (jv & ~(1 << place)) | (side << place)
                x1, r1 = place_of(io, k1, anchor[0], anchor[2])
                x2, r2 = place_of(jo, k2, anchor[1], anchor[3])
                d1, d2 = lanes_ref[level - 1, 2:3, :], lanes_ref[level - 1, 3:4, :]
                out = angle_of(speed, x1, r1, x2, r2, d1, d2)
                angle = -out if angle is None else angle - out
            sine, cosine = sine_cosine(angle)
            rows = pl.ds(pl.multiple_of(j * 16 + 8 * half, 8), 8)
            if level < 8:
                sine_r = pltpu.roll(sine, 64, 1)
                cosine_r = pltpu.roll(cosine, 64, 1)
                cos_ref[level, 0, rows, :] = jnp.where(upper, cosine_r, cosine)
                cos_ref[level, 1, rows, :] = jnp.where(upper, cosine, cosine_r)
                sin_ref[level, 0, rows, :] = jnp.where(upper, sine_r, -sine)
                sin_ref[level, 1, rows, :] = jnp.where(upper, sine, -sine_r)
            else:
                cos_ref[level, 0, rows, :] = cosine
                sin_ref[level, 0, rows, :] = jnp.where(upper, sine, -sine)
        return carry

    lax.fori_loop(0, 16, step, 0)


def spread(table, level, side, rows):
    return jnp.concatenate(
        [jnp.broadcast_to(table[level, side, pl.ds(r, 1), :], (8, 128)) for r in rows], axis=0
    )


def halves(value):
    high = value.astype(BF16)
    low = (value - high.astype(F32)).astype(BF16)
    return high, low


def merge(level, lower, upper, kids, cos_ref, sin_ref, weights):
    lower_r = pltpu.roll(lower, 64, 1)
    upper_r = pltpu.roll(upper, 64, 1)
    blocks = []
    for rows in kids:
        low = lower * spread(cos_ref, level, 0, rows) + lower_r * spread(sin_ref, level, 0, rows)
        up = upper * spread(cos_ref, level, 1, rows) + upper_r * spread(sin_ref, level, 1, rows)
        blocks.append((halves(low), halves(up)))
    high = jnp.concatenate([jnp.concatenate([b[0][0], b[1][0]], axis=1) for b in blocks], axis=0)
    rest = jnp.concatenate([jnp.concatenate([b[0][1], b[1][1]], axis=1) for b in blocks], axis=0)
    both = jnp.dot(high, weights, preferred_element_type=F32)
    both = both + jnp.dot(rest, weights, preferred_element_type=F32)
    return both[:, :128] + both[:, 128:]


def levels_kernel(speed_ref, offset_ref, lanes_ref, basis_ref, in_ref, out_ref, data, cos_ref, sin_ref):
    me = lax.axis_index("src") * lax.axis_size("tgt") + lax.axis_index("tgt")
    group = me * 8 // 32
    anchor = [offset_ref[group, c] for c in range(4)]
    speed = [speed_ref[a, b] for a in range(2) for b in range(3)]
    for level in range(9):
        make_tables(level, speed, anchor, lanes_ref, cos_ref, sin_ref)

    def load(j, carry):
        for s in range(8):
            data[j, 2 * s : 2 * s + 2] = in_ref[s, j]
        return carry

    lax.fori_loop(0, 16, load, 0)

    for level in range(8):
        place = merge_place(level)
        weights = basis_ref[level % 2]
        if level % 2 == 0:

            def step(jj, carry, level=level, place=place, weights=weights):
                low_i = [i for i in range(16) if not i >> place & 1]
                js = [2 * jj, 2 * jj + 1]
                lower = jnp.concatenate([data[j, i] for j in js for i in low_i], axis=0)
                upper = jnp.concatenate([data[j, i + (1 << place)] for j in js for i in low_i], axis=0)
                kids = [[j * 16 + i + (c << place) for j in js for i in low_i] for c in range(2)]
                result = merge(level, lower, upper, kids, cos_ref, sin_ref, weights)
                at = 0
                for c in range(2):
                    for j in js:
                        for i in low_i:
                            data[j, i + (c << place)] = result[at : at + 8]
                            at += 8
                return carry

            lax.fori_loop(0, 8, step, 0)
        else:

            def step(jj, carry, level=level, place=place, weights=weights):
                j0 = (jj >> place) * (2 << place) + (jj & ((1 << place) - 1))
                j1 = j0 + (1 << place)
                lower = jnp.concatenate([data[j0, i] for i in range(16)], axis=0)
                upper = jnp.concatenate([data[j1, i] for i in range(16)], axis=0)
                kids = [[j * 16 + i for i in range(16)] for j in (j0, j1)]
                result = merge(level, lower, upper, kids, cos_ref, sin_ref, weights)
                at = 0
                for j in (j0, j1):
                    for i in range(16):
                        block = result[at : at + 8]
                        at += 8
                        if level < 7:
                            data[j, i] = block
                        else:
                            row = [j * 16 + i]
                            out_ref[i, j] = block * spread(cos_ref, 8, 0, row) + pltpu.roll(
                                block, 64, 1
                            ) * spread(sin_ref, 8, 0, row)
                return carry

            lax.fori_loop(0, 8, step, 0)


def on_device(source_weights, wave_speed, offsets):
    widened = source_weights.astype(F32)
    received = lax.all_to_all(widened, ("src", "tgt"), split_axis=2, concat_axis=0, tiled=True)
    received = received.reshape(8, 16, 2, 8, 128)
    vmem = pl.BlockSpec(memory_space=pltpu.VMEM)
    smem = pl.BlockSpec(memory_space=pltpu.SMEM)
    return pl.pallas_call(
        levels_kernel,
        out_shape=jax.ShapeDtypeStruct((16, 16, 8, 128), F32),
        in_specs=[smem, smem, vmem, vmem, vmem],
        out_specs=vmem,
        scratch_shapes=[
            pltpu.VMEM((16, 16, 8, 128), F32),
            pltpu.VMEM((9, 2, 256, 128), F32),
            pltpu.VMEM((9, 2, 256, 128), F32),
        ],
        compiler_params=pltpu.CompilerParams(vmem_limit_bytes=48 << 20),
    )(wave_speed, offsets, jnp.asarray(lane_tables()), jnp.asarray(basis_split()), received)


def solution(mesh):
    in_specs = (P("src", "tgt", None, None), P(), P())
    out_specs = P(None, None, ("src", "tgt"), None)
    return jax.shard_map(
        on_device, mesh=mesh, in_specs=in_specs, out_specs=out_specs, check_vma=False
    )
```

```python
import functools
import math

import jax
import jax.numpy as jnp
import numpy as np
from jax import lax
from jax.experimental import pallas as pl
from jax.experimental.pallas import tpu as pltpu
from jax.sharding import PartitionSpec as P

POINTS = 8
HALF_SCALE = 2048.0
MESH = pl.DeviceIdType.MESH
F32 = jnp.float32
BF16 = jnp.bfloat16


def nodes():
    return 0.5 - 0.5 * np.cos((2.0 * np.arange(8) + 1.0) * (math.pi / 16.0))


def basis(axis):
    z = nodes()
    out = np.zeros((2, 2, 8, 8, 2, 8, 8))
    for s in range(2):
        for p in range(8):
            u = (s + z[p]) / 2.0
            for t in range(8):
                value = 1.0
                for a in range(8):
                    if a != t:
                        value *= (u - z[a]) / (z[t] - z[a])
                for h in range(2):
                    for q in range(8):
                        if axis == 0:
                            out[s, h, p, q, h, t, q] = value
                        else:
                            out[s, h, q, p, h, q, t] = value
    return out.reshape(256, 128)


def basis_split():
    both = []
    for axis in range(2):
        full = basis(axis).astype(np.float32)
        high = full.astype(jnp.bfloat16)
        low = (full - high.astype(np.float32)).astype(jnp.bfloat16)
        both.append(np.concatenate([high, high, low], axis=0))
    return np.stack(both)


def lane_tables():
    z = nodes().astype(np.float32)
    lane = np.arange(128)
    s, p1, p2 = lane // 64, lane // 8 % 8, lane % 8
    out = np.zeros((8, 4, 128), np.float32)
    for level in range(8):
        k1, k2 = level // 2 + 1, (level + 1) // 2
        w1, w2 = np.float32(2.0 ** (k1 - 10)), np.float32(2.0 ** (k2 - 10))
        if level % 2 == 0:
            out[level, 0] = w1 / 2 * (s.astype(np.float32) + z[p1])
            out[level, 1] = w2 * z[p2]
        else:
            out[level, 0] = w1 * z[p1]
            out[level, 1] = w2 / 2 * (s.astype(np.float32) + z[p2])
        out[level, 2] = w1 * z[p1]
        out[level, 3] = w2 * z[p2]
    return out


def sine_cosine(half):
    turns = half * (1.0 / math.pi) + 12582912.0
    turns = turns - 12582912.0
    rest = half - turns * 3.140625
    rest = rest - turns * 9.67653589793e-4
    sq = rest * rest
    sine = ((5.1995018e-6 * sq - 3.9612958e-4) * sq + 1.66660308e-2) * sq - 3.3333314e-1
    sine = (sine * sq + 2.0) * rest
    cosine = (2.337661e-5 * sq - 1.3865138e-3) * sq + 4.1665433e-2
    cosine = (cosine * sq - 0.5) * sq + 1.0
    return sine * cosine, 1.0 - 0.5 * (sine * sine)


def source_index(box, done):
    total = box * 0
    for place in range(4 - done):
        total = total + (((box >> place) & 1) << (3 - done - place))
    return total


def part_of(box, done, target_anchor, source_anchor, slopes, shifts, delta):
    x = target_anchor + ((box >> (4 - done)).astype(F32) + 0.5) * (2.0 ** (-2 - done))
    r = source_anchor + source_index(box, done).astype(F32) * (2.0 ** (done - 10))
    first, second = slopes[0] * x, slopes[1] * x
    if shifts is not None:
        first, second = shifts[0] + first, shifts[1] + second
    k = r + delta
    scaled = delta * HALF_SCALE
    return first, second, scaled * (k + r), k * k, r * r, x * scaled


def half_angle(one, two):
    s1, s2 = one[0] + two[0], one[1] + two[1]
    a1, a2 = s1 * s1, s2 * s2
    over = a1 * one[2] + a2 * two[2]
    there = a1 * one[3] + a2 * two[3]
    here = a1 * one[4] + a2 * two[4]
    under = there * lax.rsqrt(there) + here * lax.rsqrt(here)
    return (one[5] + two[5]) + over / under


def merge_place(level):
    return 3 - level // 2


def make_tables(level, speed, anchor, lanes_ref, cos_ref, sin_ref):
    lane = lax.broadcasted_iota(jnp.int32, (8, 128), 1)
    row = lax.broadcasted_iota(jnp.int32, (8, 128), 0)
    upper = lane >= 64
    side = jnp.where(upper, 1, 0)
    place = merge_place(level)
    low = (1 << place) - 1 if level < 8 else 0

    def first(box, at, which):
        return part_of(
            box, at // 2 + 1, anchor[0], anchor[2], (speed[1], speed[4]), (speed[0], speed[3]),
            lanes_ref[at, which : which + 1, :],
        )

    def second(box, at, which):
        return part_of(
            box, (at + 1) // 2, anchor[1], anchor[3], (speed[2], speed[5]), None,
            lanes_ref[at, which : which + 1, :],
        )

    def store(angle, at):
        sine, cosine = sine_cosine(angle)
        rows = pl.ds(pl.multiple_of(at, 8), 8)
        if level < 8:
            sine_r = pltpu.roll(sine, 64, 1)
            cosine_r = pltpu.roll(cosine, 64, 1)
            cos_ref[level, 0, rows, :] = jnp.where(upper, cosine_r, cosine)
            cos_ref[level, 1, rows, :] = jnp.where(upper, cosine, cosine_r)
            sin_ref[level, 0, rows, :] = jnp.where(upper, sine_r, -sine)
            sin_ref[level, 1, rows, :] = jnp.where(upper, sine, -sine_r)
        else:
            cos_ref[level, 0, rows, :] = cosine
            sin_ref[level, 0, rows, :] = jnp.where(upper, sine, -sine)

    if level == 8:
        ones = [first(row + 8 * half, 7, 2) for half in range(2)]

        def step(jj, carry):
            for j in (2 * jj, 2 * jj + 1):
                two = second(j, 7, 3)
                for half in range(2):
                    store(-half_angle(ones[half], two), j * 16 + 8 * half)
            return carry

    elif level % 2 == 0:
        pair = ((row & ~low) << 1) | (row & low)
        ones = [first(pair | (c << place), level, 0) for c in range(2)]
        if level > 0:
            outs = first(pair | (side << place), level - 1, 2)

        def step(jj, carry):
            for j in (2 * jj, 2 * jj + 1):
                two = second(j, level, 1)
                if level > 0:
                    out = half_angle(outs, second(j, level - 1, 3))
                for c in range(2):
                    angle = half_angle(ones[c], two)
                    if level > 0:
                        angle = angle - out
                    store(angle, j * 16 + 8 * c)
            return carry

    else:
        ones = [first(row + 8 * half, level, 0) for half in range(2)]
        outs = [first(row + 8 * half, level - 1, 2) for half in range(2)]

        def step(jj, carry):
            j0 = ((jj >> place) << (place + 1)) | (jj & low)
            two_out = second(j0 + (side << place), level - 1, 3)
            out = [half_angle(outs[half], two_out) for half in range(2)]
            for c in range(2):
                j = j0 + (c << place)
                two = second(j, level, 1)
                for half in range(2):
                    store(half_angle(ones[half], two) - out[half], j * 16 + 8 * half)
            return carry

    lax.fori_loop(0, 8, step, 0)


def spread(table, level, side, rows):
    return jnp.concatenate(
        [jnp.broadcast_to(table[level, side, pl.ds(r, 1), :], (8, 128)) for r in rows], axis=0
    )


def halves(value):
    high = value.astype(BF16)
    low = (value - high.astype(F32)).astype(BF16)
    return high, low


def merge(level, lower, upper, kids, cos_ref, sin_ref, weights):
    lower_r = pltpu.roll(lower, 64, 1)
    upper_r = pltpu.roll(upper, 64, 1)
    blocks = []
    for rows in kids:
        low = lower * spread(cos_ref, level, 0, rows) + lower_r * spread(sin_ref, level, 0, rows)
        up = upper * spread(cos_ref, level, 1, rows) + upper_r * spread(sin_ref, level, 1, rows)
        (low_h, low_r), (up_h, up_r) = halves(low), halves(up)
        blocks.append(jnp.concatenate([low_h, up_h, low_r, up_r, low_h, up_h], axis=1))
    return jnp.dot(jnp.concatenate(blocks, axis=0), weights, preferred_element_type=F32)


def merge_first(level, js, data, cos_ref, sin_ref, basis_ref):
    place = merge_place(level)
    low_i = [i for i in range(16) if not i >> place & 1]
    high_i = [i + (1 << place) for i in low_i]
    lower = jnp.concatenate([data[j, i] for j in js for i in low_i], axis=0)
    upper = jnp.concatenate([data[j, i] for j in js for i in high_i], axis=0)
    kids = [[j * 16 + 8 * c + p for j in js for p in range(8)] for c in range(2)]
    result = merge(level, lower, upper, kids, cos_ref, sin_ref, basis_ref[0])
    at = 0
    for into in (low_i, high_i):
        for j in js:
            for i in into:
                data[j, i] = result[at : at + 8]
                at += 8


def merge_second(level, pairs, data, cos_ref, sin_ref, basis_ref, out_ref=None):
    lower = jnp.concatenate([data[j0, i] for j0, _ in pairs for i in range(16)], axis=0)
    upper = jnp.concatenate([data[j1, i] for _, j1 in pairs for i in range(16)], axis=0)
    kids = [[pair[c] * 16 + i for pair in pairs for i in range(16)] for c in range(2)]
    result = merge(level, lower, upper, kids, cos_ref, sin_ref, basis_ref[1])
    at = 0
    for c in range(2):
        for pair in pairs:
            for i in range(16):
                block = result[at : at + 8]
                at += 8
                if out_ref is None:
                    data[pair[c], i] = block
                else:
                    row = [pair[c] * 16 + i]
                    out_ref[i, pair[c]] = block * spread(cos_ref, 8, 0, row) + pltpu.roll(
                        block, 64, 1
                    ) * spread(sin_ref, 8, 0, row)


def kernel(speed_ref, offset_ref, lanes_hbm, basis_hbm, in_hbm, out_ref,
           narrow, wide, data, cos_ref, sin_ref, lanes_ref, basis_ref, load_sem, send_sem, recv_sem):
    src, tgt = lax.axis_index("src"), lax.axis_index("tgt")
    me = src * 16 + tgt
    n = 128

    def peer(a, b):
        return lax.rem(src + a, 8), lax.rem(tgt + b, 16)

    barrier = pltpu.get_barrier_semaphore()
    for a in range(8):
        for b in range(16):
            if a or b:
                pl.semaphore_signal(barrier, inc=1, device_id=peer(a, b), device_id_type=MESH)
    loads = [
        pltpu.make_async_copy(in_hbm, narrow, load_sem.at[0]),
        pltpu.make_async_copy(lanes_hbm, lanes_ref, load_sem.at[1]),
        pltpu.make_async_copy(basis_hbm, basis_ref, load_sem.at[2]),
    ]
    for load in loads:
        load.start()
    loads[0].wait()

    def widen(q, carry):
        cols = pl.ds(pl.multiple_of(q * 32, 32), 32)
        for r in range(2):
            rows = narrow[r, cols, :].astype(F32)
            for c in range(4):
                wide[q * 4 + c, r] = rows[8 * c : 8 * c + 8]
        return carry

    lax.fori_loop(0, n // 4, widen, 0)
    pl.semaphore_wait(barrier, n - 1)

    pltpu.make_async_copy(wide.at[me], data.at[tgt, src], recv_sem.at[0]).start()

    def send(a, b):
        to = peer(a, b)
        pltpu.make_async_remote_copy(
            src_ref=wide.at[to[0] * 16 + to[1]],
            dst_ref=data.at[tgt, src],
            send_sem=send_sem,
            recv_sem=recv_sem.at[b],
            device_id=to,
            device_id_type=MESH,
        ).start()

    for b in (0, 8, 4, 12, 2, 10, 6, 14, 1, 9, 5, 13, 3, 11, 7, 15):
        for a in range(8):
            if a or b:
                send(a, b)

    loads[1].wait()
    loads[2].wait()
    group = me * 8 // 32
    anchor = [offset_ref[group, c] for c in range(4)]
    speed = [speed_ref[a, b] for a in range(2) for b in range(3)]
    for level in range(9):
        make_tables(level, speed, anchor, lanes_ref, cos_ref, sin_ref)

    boxes = data.reshape(16, 16, 8, 128)
    args = (boxes, cos_ref, sin_ref, basis_ref)

    def eighth(b):
        for part in (b, b + 8):
            here = data.at[lax.rem(tgt - part + 16, 16)]
            pltpu.make_async_copy(here, here, recv_sem.at[part]).wait()
        j0 = lax.rem(tgt - b + 16, 8)
        merge_first(0, [j0, j0 + 8], *args)
        merge_second(1, [(j0, j0 + 8)], *args)
        merge_first(2, [j0, j0 + 8], *args)

    def quarter(b):
        def step(p, carry):
            eighth(b + 4 * p)
            return carry

        lax.fori_loop(0, 2, step, 0)
        j0 = lax.rem(tgt - b + 16, 4)
        merge_second(3, [(j0, j0 + 4), (j0 + 8, j0 + 12)], *args)
        merge_first(4, [j0, j0 + 4, j0 + 8, j0 + 12], *args)

    def half(b, carry):
        def step(q, carry):
            quarter(b + 2 * q)
            return carry

        lax.fori_loop(0, 2, step, 0)
        j0 = lax.rem(tgt - b + 16, 2)

        def five(k, carry):
            j = j0 + 8 * k
            merge_second(5, [(j, j + 2), (j + 4, j + 6)], *args)
            return carry

        def six(k, carry):
            j = j0 + 8 * k
            merge_first(6, [j, j + 2, j + 4, j + 6], *args)
            return carry

        lax.fori_loop(0, 2, five, 0)
        lax.fori_loop(0, 2, six, 0)
        return carry

    lax.fori_loop(0, 2, half, 0)

    def seven(k, carry):
        merge_second(7, [(4 * k, 4 * k + 1), (4 * k + 2, 4 * k + 3)], *args, out_ref=out_ref)
        return carry

    lax.fori_loop(0, 4, seven, 0)
    sent = wide.at[pl.ds(0, n - 1)]
    pltpu.make_async_copy(sent, sent, send_sem).wait()


def on_device(source_weights, wave_speed, offsets):
    vmem = pl.BlockSpec(memory_space=pltpu.VMEM)
    smem = pl.BlockSpec(memory_space=pltpu.SMEM)
    anywhere = pl.BlockSpec(memory_space=pl.ANY)
    return pl.pallas_call(
        kernel,
        out_shape=jax.ShapeDtypeStruct((16, 16, 8, 128), F32),
        in_specs=[smem, smem, anywhere, anywhere, anywhere],
        out_specs=vmem,
        scratch_shapes=[
            pltpu.VMEM((2, 1024, 128), BF16),
            pltpu.VMEM((128, 2, 8, 128), F32),
            pltpu.VMEM((16, 8, 2, 8, 128), F32),
            pltpu.VMEM((9, 2, 256, 128), F32),
            pltpu.VMEM((9, 2, 256, 128), F32),
            pltpu.VMEM((8, 4, 128), F32),
            pltpu.VMEM((2, 768, 128), BF16),
            pltpu.SemaphoreType.DMA((3,)),
            pltpu.SemaphoreType.DMA,
            pltpu.SemaphoreType.DMA((16,)),
        ],
        compiler_params=pltpu.CompilerParams(
            collective_id=0, has_side_effects=True, vmem_limit_bytes=48 << 20
        ),
    )(
        wave_speed,
        offsets,
        jnp.asarray(lane_tables()),
        jnp.asarray(basis_split()),
        source_weights.reshape(2, 1024, 128),
    )


def solution(mesh):
    in_specs = (P("src", "tgt", None, None), P(), P())
    out_specs = P(None, None, ("src", "tgt"), None)
    return jax.shard_map(
        on_device, mesh=mesh, in_specs=in_specs, out_specs=out_specs, check_vma=False
    )
```

```python
import functools
import math

import jax
import jax.numpy as jnp
import numpy as np
from jax import lax
from jax.experimental import pallas as pl
from jax.experimental.pallas import tpu as pltpu
from jax.sharding import PartitionSpec as P

POINTS = 8
HALF_SCALE = 2048.0
VMEM_BYTES = 48 << 20
AHEAD = 56
FIRST = 2
MESH = pl.DeviceIdType.MESH
F32 = jnp.float32
BF16 = jnp.bfloat16


def node_values():
    return [float(v) for v in 0.5 - 0.5 * np.cos((2.0 * np.arange(8) + 1.0) * (math.pi / 16.0))]


def pick(index, values):
    result = jnp.full(index.shape, values[0], F32)
    for at in range(1, len(values)):
        result = jnp.where(index == at, values[at], result)
    return result


def make_basis(axis, basis_ref):
    z = node_values()
    gaps = [math.prod(z[t] - z[a] for a in range(8) if a != t) for t in range(8)]
    col = lax.broadcasted_iota(jnp.int32, (16, 128), 1)

    def step(k, carry):
        row = lax.broadcasted_iota(jnp.int32, (16, 128), 0) + k * 16
        row_points, col_points = ((row >> 3) & 7, row & 7), ((col >> 3) & 7, col & 7)
        t = col_points[axis]
        u = ((row >> 7).astype(F32) + pick(row_points[axis], z)) * 0.5
        value = 1.0 / pick(t, gaps)
        for at in range(8):
            value = value * jnp.where(t == at, 1.0, u - z[at])
        same = (row_points[1 - axis] == col_points[1 - axis]) & (((row >> 6) & 1) == (col >> 6))
        high, low = halves(jnp.where(same, value, 0.0))
        rows = pl.ds(pl.multiple_of(k * 16, 16), 16)
        basis_ref[axis, rows, 0:128] = high
        basis_ref[axis, rows, 128:256] = low
        return carry

    lax.fori_loop(0, 16, step, 0)


def displacement(level, which):
    z = node_values()
    lane = lax.broadcasted_iota(jnp.int32, (8, 128), 1)
    dim = which % 2
    width = 2.0 ** ((level // 2 + 1, (level + 1) // 2)[dim] - 10)
    point = pick((lane & 7) if dim else ((lane >> 3) & 7), z)
    if which < 2 and level % 2 == dim:
        return (point + (lane >> 6).astype(F32)) * (width / 2)
    return point * width


def sine_cosine(half):
    turns = half * (1.0 / math.pi) + 12582912.0
    turns = turns - 12582912.0
    rest = half - turns * 3.140625
    rest = rest - turns * 9.67653589793e-4
    sq = rest * rest
    sine = ((5.1995018e-6 * sq - 3.9612958e-4) * sq + 1.66660308e-2) * sq - 3.3333314e-1
    sine = (sine * sq + 2.0) * rest
    cosine = (2.337661e-5 * sq - 1.3865138e-3) * sq + 4.1665433e-2
    cosine = (cosine * sq - 0.5) * sq + 1.0
    return sine * cosine, 1.0 - 0.5 * (sine * sine)


def source_index(box, done):
    total = box * 0
    for place in range(4 - done):
        total = total + (((box >> place) & 1) << (3 - done - place))
    return total


def part_of(box, done, target_anchor, source_anchor, slopes, shifts, delta):
    x = target_anchor + ((box >> (4 - done)).astype(F32) + 0.5) * (2.0 ** (-2 - done))
    r = source_anchor + source_index(box, done).astype(F32) * (2.0 ** (done - 10))
    first, second = slopes[0] * x, slopes[1] * x
    if shifts is not None:
        first, second = shifts[0] + first, shifts[1] + second
    k = r + delta
    scaled = delta * HALF_SCALE
    return first, second, scaled * (k + r), k * k, r * r, x * scaled


def half_angle(one, two):
    s1, s2 = one[0] + two[0], one[1] + two[1]
    a1, a2 = s1 * s1, s2 * s2
    over = a1 * one[2] + a2 * two[2]
    there = a1 * one[3] + a2 * two[3]
    here = a1 * one[4] + a2 * two[4]
    under = there * lax.rsqrt(there) + here * lax.rsqrt(here)
    return (one[5] + two[5]) + over / under


def merge_place(level):
    return 3 - level // 2


def make_tables(level, speed, anchor, cos_ref, sin_ref):
    lane = lax.broadcasted_iota(jnp.int32, (8, 128), 1)
    row = lax.broadcasted_iota(jnp.int32, (8, 128), 0)
    upper = lane >= 64
    side = jnp.where(upper, 1, 0)
    place = merge_place(level)
    low = (1 << place) - 1 if level < 8 else 0

    def first(box, at, which):
        return part_of(
            box, at // 2 + 1, anchor[0], anchor[2], (speed[1], speed[4]), (speed[0], speed[3]),
            displacement(at, which),
        )

    def second(box, at, which):
        return part_of(
            box, (at + 1) // 2, anchor[1], anchor[3], (speed[2], speed[5]), None,
            displacement(at, which),
        )

    def store(angle, at):
        sine, cosine = sine_cosine(angle)
        rows = pl.ds(pl.multiple_of(at, 8), 8)
        cos_ref[level, 0, rows, :] = cosine
        sin_ref[level, 0, rows, :] = sine if level < 8 else jnp.where(upper, sine, -sine)

    if level == 8:
        ones = [first(row + 8 * half, 7, 2) for half in range(2)]

        def step(jj, carry):
            for j in (2 * jj, 2 * jj + 1):
                two = second(j, 7, 3)
                for half in range(2):
                    store(-half_angle(ones[half], two), j * 16 + 8 * half)
            return carry

    elif level % 2 == 0:
        pair = ((row & ~low) << 1) | (row & low)
        ones = [first(pair | (c << place), level, 0) for c in range(2)]
        if level > 0:
            outs = first(pair | (side << place), level - 1, 2)

        def step(jj, carry):
            for j in (2 * jj, 2 * jj + 1):
                two = second(j, level, 1)
                if level > 0:
                    out = half_angle(outs, second(j, level - 1, 3))
                for c in range(2):
                    angle = half_angle(ones[c], two)
                    if level > 0:
                        angle = angle - out
                    store(angle, j * 16 + 8 * c)
            return carry

    else:
        ones = [first(row + 8 * half, level, 0) for half in range(2)]
        outs = [first(row + 8 * half, level - 1, 2) for half in range(2)]

        def step(jj, carry):
            j0 = ((jj >> place) << (place + 1)) | (jj & low)
            two_out = second(j0 + (side << place), level - 1, 3)
            out = [half_angle(outs[half], two_out) for half in range(2)]
            for c in range(2):
                j = j0 + (c << place)
                two = second(j, level, 1)
                for half in range(2):
                    store(half_angle(ones[half], two) - out[half], j * 16 + 8 * half)
            return carry

    lax.fori_loop(0, 8, step, 0)
    if level == 8:
        return

    def widen(k, carry):
        rows = [pl.ds(pl.multiple_of(k * 64 + 8 * q, 8), 8) for q in range(8)]
        sines = [sin_ref[level, 0, r, :] for r in rows]
        cosines = [cos_ref[level, 0, r, :] for r in rows]
        sines_r = [pltpu.roll(v, 64, 1) for v in sines]
        cosines_r = [pltpu.roll(v, 64, 1) for v in cosines]
        for r, sine, cosine, sine_r, cosine_r in zip(rows, sines, cosines, sines_r, cosines_r):
            cos_ref[level, 0, r, :] = jnp.where(upper, cosine_r, cosine)
            cos_ref[level, 1, r, :] = jnp.where(upper, cosine, cosine_r)
            sin_ref[level, 0, r, :] = jnp.where(upper, sine_r, -sine)
            sin_ref[level, 1, r, :] = jnp.where(upper, sine, -sine_r)
        return carry

    lax.fori_loop(0, 4, widen, 0)


def spread(table, level, side, rows):
    return jnp.concatenate(
        [jnp.broadcast_to(table[level, side, pl.ds(r, 1), :], (8, 128)) for r in rows], axis=0
    )


def halves(value):
    high = value.astype(BF16)
    low = (value - high.astype(F32)).astype(BF16)
    return high, low


def merge(level, tiles, js, cos_ref, sin_ref, basis_ref):
    place = merge_place(level)
    count = len(js)
    low = 1 << place
    if level % 2 == 0:
        starts = [i for i in range(16) if not i & low]
        pairs = [((k, i), (k, i + low)) for k in range(count) for i in starts]
        rows = [[js[k] * 16 + 8 * c + p for k in range(count) for p in range(8)] for c in range(2)]
    else:
        apart = low * count // 16
        firsts = [k for k in range(count) if not k & apart]
        pairs = [((k, i), (k + apart, i)) for k in firsts for i in range(16)]
        rows = [[js[k + c * apart] * 16 + i for k in firsts for i in range(16)] for c in range(2)]
    lower = jnp.concatenate([tiles[p] for p, _ in pairs], axis=0)
    upper = jnp.concatenate([tiles[q] for _, q in pairs], axis=0)
    lower_r = pltpu.roll(lower, 64, 1)
    upper_r = pltpu.roll(upper, 64, 1)
    high, rest = [], []
    for kid in rows:
        down = lower * spread(cos_ref, level, 0, kid) + lower_r * spread(sin_ref, level, 0, kid)
        up = upper * spread(cos_ref, level, 1, kid) + upper_r * spread(sin_ref, level, 1, kid)
        (down_h, down_r), (up_h, up_r) = halves(down), halves(up)
        high.append(jnp.concatenate([down_h, up_h], axis=1))
        rest.append(jnp.concatenate([down_r, up_r], axis=1))
    weights = basis_ref[level % 2]
    both = jnp.dot(jnp.concatenate(high, axis=0), weights, preferred_element_type=F32)
    both = both + jnp.dot(jnp.concatenate(rest, axis=0), weights, preferred_element_type=F32)
    result = both[:, :128] + both[:, 128:]
    after = [p for p, _ in pairs] + [q for _, q in pairs]
    return {at: result[8 * n : 8 * n + 8] for n, at in enumerate(after)}


def kernel(speed_hbm, offset_hbm, in_hbm, out_ref, speed_ref, offset_ref,
           narrow, wide, data, cos_ref, sin_ref, basis_ref, load_sem, send_sem, recv_sem):
    src, tgt = lax.axis_index("src"), lax.axis_index("tgt")
    me = src * 16 + tgt
    n = 128

    def peer(a, b):
        return lax.rem(src + a, 8), lax.rem(tgt + b, 16)

    loads = [
        pltpu.make_async_copy(in_hbm, narrow, load_sem.at[0]),
        pltpu.make_async_copy(speed_hbm, speed_ref, load_sem.at[1]),
        pltpu.make_async_copy(offset_hbm, offset_ref, load_sem.at[2]),
    ]
    for load in loads:
        load.start()
    barrier = pltpu.get_barrier_semaphore()
    for a in range(8):
        for b in range(16):
            if a or b:
                pl.semaphore_signal(barrier, inc=1, device_id=peer(a, b), device_id_type=MESH)
    for load in loads:
        load.wait()

    def widen(q, carry):
        cols = pl.ds(pl.multiple_of(q * 32, 32), 32)
        for r in range(2):
            rows = narrow[r, cols, :].astype(F32)
            for c in range(4):
                wide[q * 4 + c, r] = rows[8 * c : 8 * c + 8]
        return carry

    lax.fori_loop(0, n // 4, widen, 0)
    entry = 4 * (src // 2) + 5 * (src % 2 + 2 * (tgt // 8)) + 8 * (tgt // 2 % 4)
    ahead = lax.div(AHEAD - entry, 6)

    group = me * 8 // 32
    anchor = [offset_ref[c, group] for c in range(4)]
    speed = [speed_ref[a, b] for a in range(2) for b in range(3)]

    def table(level, wanted):
        @pl.when(wanted)
        def _():
            make_tables(level, speed, anchor, cos_ref, sin_ref)

    for level in range(9):
        table(level, level < ahead)
    pl.semaphore_wait(barrier, n - 1)

    pltpu.make_async_copy(wide.at[me], data.at[tgt, src], recv_sem.at[0]).start()

    def send(a, b):
        to = peer(a, b)
        pltpu.make_async_remote_copy(
            src_ref=wide.at[to[0] * 16 + to[1]],
            dst_ref=data.at[tgt, src],
            send_sem=send_sem,
            recv_sem=recv_sem.at[b],
            device_id=to,
            device_id_type=MESH,
        ).start()

    def send_eighth(k):
        for b in (k, k + 8):
            for a in range(8):
                if a or b:
                    send(a, b)

    order = (0, 4, 2, 6, 1, 5, 3, 7)
    for k in order[:FIRST]:
        send_eighth(k)
    for level in range(9):
        table(level, level >= ahead)
        for k in order[FIRST + level : FIRST + level + 1]:
            send_eighth(k)
    for axis in range(2):
        make_basis(axis, basis_ref)

    boxes = data.reshape(16, 16, 8, 128)
    tables = (cos_ref, sin_ref, basis_ref)

    def quarter(q, carry):
        b = lax.rem(q, 2) * 2 + q // 2
        for part in (b, b + 8, b + 4, b + 12):
            here = data.at[lax.rem(tgt - part + 16, 16)]
            pltpu.make_async_copy(here, here, recv_sem.at[part]).wait()
        j0 = lax.rem(tgt - b + 16, 4)
        js = [j0 + 4 * k for k in range(4)]
        tiles = {(k, i): boxes[js[k], i] for k in range(4) for i in range(16)}
        for level in range(5):
            tiles = merge(level, tiles, js, *tables)
        for (k, i), value in tiles.items():
            boxes[js[k], i] = value
        return carry

    def half(b, carry):
        lax.fori_loop(2 * b, 2 * b + 2, quarter, 0)
        j0 = lax.rem(tgt - b + 16, 2)
        js = [j0 + 2 * k for k in range(8)]
        tiles = {(k, i): boxes[js[k], i] for k in range(8) for i in range(16)}
        for level in (5, 6):
            tiles = merge(level, tiles, js, *tables)
        for (k, i), value in tiles.items():
            boxes[js[k], i] = value
        return carry

    lax.fori_loop(0, 2, half, 0)
    js = list(range(16))
    tiles = {(k, i): boxes[k, i] for k in js for i in range(16)}
    tiles = merge(7, tiles, js, *tables)
    for k in js:
        block = jnp.concatenate([tiles[k, i] for i in range(16)], axis=0)
        rows = [k * 16 + i for i in range(16)]
        block = block * spread(cos_ref, 8, 0, rows) + pltpu.roll(block, 64, 1) * spread(
            sin_ref, 8, 0, rows
        )
        for i in range(16):
            out_ref[i, k] = block[8 * i : 8 * i + 8]
    sent = wide.at[pl.ds(0, n - 1)]
    pltpu.make_async_copy(sent, sent, send_sem).wait()


def on_device(source_weights, wave_speed, offsets):
    vmem = pl.BlockSpec(memory_space=pltpu.VMEM)
    anywhere = pl.BlockSpec(memory_space=pltpu.HBM)
    return pl.pallas_call(
        kernel,
        out_shape=jax.ShapeDtypeStruct((16, 16, 8, 128), F32),
        in_specs=[anywhere, anywhere, anywhere],
        out_specs=vmem,
        scratch_shapes=[
            pltpu.SMEM((2, 3), F32),
            pltpu.SMEM((4, 32), F32),
            pltpu.VMEM((2, 1024, 128), BF16),
            pltpu.VMEM((128, 2, 8, 128), F32),
            pltpu.VMEM((16, 8, 2, 8, 128), F32),
            pltpu.VMEM((9, 2, 256, 128), F32),
            pltpu.VMEM((9, 2, 256, 128), F32),
            pltpu.VMEM((2, 256, 256), BF16),
            pltpu.SemaphoreType.DMA((3,)),
            pltpu.SemaphoreType.DMA,
            pltpu.SemaphoreType.DMA((16,)),
        ],
        compiler_params=pltpu.CompilerParams(
            collective_id=0, has_side_effects=True, vmem_limit_bytes=VMEM_BYTES
        ),
    )(wave_speed, offsets.T, source_weights.reshape(2, 1024, 128))


def solution(mesh):
    in_specs = (P("src", "tgt", None, None), P(), P())
    out_specs = P(None, None, ("src", "tgt"), None)
    return jax.shard_map(
        on_device, mesh=mesh, in_specs=in_specs, out_specs=out_specs, check_vma=False
    )
```

```python
import functools
import math

import jax
import jax.numpy as jnp
import numpy as np
from jax import lax
from jax.experimental import pallas as pl
from jax.experimental.pallas import tpu as pltpu
from jax.sharding import PartitionSpec as P

POINTS = 8
HALF_SCALE = 2048.0
VMEM_BYTES = 48 << 20
AHEAD = 56
MESH = pl.DeviceIdType.MESH
F32 = jnp.float32
BF16 = jnp.bfloat16


def node_values():
    return [float(v) for v in 0.5 - 0.5 * np.cos((2.0 * np.arange(8) + 1.0) * (math.pi / 16.0))]


def pick(index, values):
    result = jnp.full(index.shape, values[0], F32)
    for at in range(1, len(values)):
        result = jnp.where(index == at, values[at], result)
    return result


def make_basis(axis, basis_ref):
    z = node_values()
    gaps = [math.prod(z[t] - z[a] for a in range(8) if a != t) for t in range(8)]
    col = lax.broadcasted_iota(jnp.int32, (16, 128), 1)

    def step(k, carry):
        row = lax.broadcasted_iota(jnp.int32, (16, 128), 0) + k * 16
        row_points, col_points = ((row >> 3) & 7, row & 7), ((col >> 3) & 7, col & 7)
        t = col_points[axis]
        u = ((row >> 7).astype(F32) + pick(row_points[axis], z)) * 0.5
        value = 1.0 / pick(t, gaps)
        for at in range(8):
            value = value * jnp.where(t == at, 1.0, u - z[at])
        same = (row_points[1 - axis] == col_points[1 - axis]) & (((row >> 6) & 1) == (col >> 6))
        high, low = halves(jnp.where(same, value, 0.0))
        rows = pl.ds(pl.multiple_of(k * 16, 16), 16)
        basis_ref[axis, rows, 0:128] = high
        basis_ref[axis, rows, 128:256] = low
        return carry

    lax.fori_loop(0, 16, step, 0)


def displacement(level, which):
    z = node_values()
    lane = lax.broadcasted_iota(jnp.int32, (8, 128), 1)
    dim = which % 2
    width = 2.0 ** ((level // 2 + 1, (level + 1) // 2)[dim] - 10)
    point = pick((lane & 7) if dim else ((lane >> 3) & 7), z)
    if which < 2 and level % 2 == dim:
        return (point + (lane >> 6).astype(F32)) * (width / 2)
    return point * width


def sine_cosine(half):
    turns = half * (1.0 / math.pi) + 12582912.0
    turns = turns - 12582912.0
    rest = half - turns * 3.140625
    rest = rest - turns * 9.67653589793e-4
    sq = rest * rest
    sine = ((5.1995018e-6 * sq - 3.9612958e-4) * sq + 1.66660308e-2) * sq - 3.3333314e-1
    sine = (sine * sq + 2.0) * rest
    cosine = (2.337661e-5 * sq - 1.3865138e-3) * sq + 4.1665433e-2
    cosine = (cosine * sq - 0.5) * sq + 1.0
    return sine * cosine, 1.0 - 0.5 * (sine * sine)


def source_index(box, done):
    total = box * 0
    for place in range(4 - done):
        total = total + (((box >> place) & 1) << (3 - done - place))
    return total


def part_of(box, done, target_anchor, source_anchor, slopes, shifts, delta):
    x = target_anchor + ((box >> (4 - done)).astype(F32) + 0.5) * (2.0 ** (-2 - done))
    r = source_anchor + source_index(box, done).astype(F32) * (2.0 ** (done - 10))
    first, second = slopes[0] * x, slopes[1] * x
    if shifts is not None:
        first, second = shifts[0] + first, shifts[1] + second
    k = r + delta
    scaled = delta * HALF_SCALE
    return first, second, scaled * (k + r), k * k, r * r, x * scaled


def half_angle(one, two):
    s1, s2 = one[0] + two[0], one[1] + two[1]
    a1, a2 = s1 * s1, s2 * s2
    over = a1 * one[2] + a2 * two[2]
    there = a1 * one[3] + a2 * two[3]
    here = a1 * one[4] + a2 * two[4]
    under = there * lax.rsqrt(there) + here * lax.rsqrt(here)
    return (one[5] + two[5]) + over / under


def merge_place(level):
    return 3 - level // 2


def make_tables(level, speed, anchor, cos_ref, sin_ref):
    lane = lax.broadcasted_iota(jnp.int32, (8, 128), 1)
    row = lax.broadcasted_iota(jnp.int32, (8, 128), 0)
    upper = lane >= 64
    side = jnp.where(upper, 1, 0)
    place = merge_place(level)
    low = (1 << place) - 1 if level < 8 else 0

    def first(box, at, which):
        return part_of(
            box, at // 2 + 1, anchor[0], anchor[2], (speed[1], speed[4]), (speed[0], speed[3]),
            displacement(at, which),
        )

    def second(box, at, which):
        return part_of(
            box, (at + 1) // 2, anchor[1], anchor[3], (speed[2], speed[5]), None,
            displacement(at, which),
        )

    def store(angle, at):
        sine, cosine = sine_cosine(angle)
        rows = pl.ds(pl.multiple_of(at, 8), 8)
        cos_ref[level, 0, rows, :] = cosine
        sin_ref[level, 0, rows, :] = sine if level < 8 else jnp.where(upper, sine, -sine)

    if level == 8:
        ones = [first(row + 8 * half, 7, 2) for half in range(2)]

        def step(jj, carry):
            for j in (2 * jj, 2 * jj + 1):
                two = second(j, 7, 3)
                for half in range(2):
                    store(-half_angle(ones[half], two), j * 16 + 8 * half)
            return carry

    elif level % 2 == 0:
        pair = ((row & ~low) << 1) | (row & low)
        ones = [first(pair | (c << place), level, 0) for c in range(2)]
        if level > 0:
            outs = first(pair | (side << place), level - 1, 2)

        def step(jj, carry):
            for j in (2 * jj, 2 * jj + 1):
                two = second(j, level, 1)
                if level > 0:
                    out = half_angle(outs, second(j, level - 1, 3))
                for c in range(2):
                    angle = half_angle(ones[c], two)
                    if level > 0:
                        angle = angle - out
                    store(angle, j * 16 + 8 * c)
            return carry

    else:
        ones = [first(row + 8 * half, level, 0) for half in range(2)]
        outs = [first(row + 8 * half, level - 1, 2) for half in range(2)]

        def step(jj, carry):
            j0 = ((jj >> place) << (place + 1)) | (jj & low)
            two_out = second(j0 + (side << place), level - 1, 3)
            out = [half_angle(outs[half], two_out) for half in range(2)]
            for c in range(2):
                j = j0 + (c << place)
                two = second(j, level, 1)
                for half in range(2):
                    store(half_angle(ones[half], two) - out[half], j * 16 + 8 * half)
            return carry

    lax.fori_loop(0, 8, step, 0)
    if level == 8:
        return

    def widen(k, carry):
        rows = [pl.ds(pl.multiple_of(k * 64 + 8 * q, 8), 8) for q in range(8)]
        sines = [sin_ref[level, 0, r, :] for r in rows]
        cosines = [cos_ref[level, 0, r, :] for r in rows]
        sines_r = [pltpu.roll(v, 64, 1) for v in sines]
        cosines_r = [pltpu.roll(v, 64, 1) for v in cosines]
        for r, sine, cosine, sine_r, cosine_r in zip(rows, sines, cosines, sines_r, cosines_r):
            cos_ref[level, 0, r, :] = jnp.where(upper, cosine_r, cosine)
            cos_ref[level, 1, r, :] = jnp.where(upper, cosine, cosine_r)
            sin_ref[level, 0, r, :] = jnp.where(upper, sine_r, -sine)
            sin_ref[level, 1, r, :] = jnp.where(upper, sine, -sine_r)
        return carry

    lax.fori_loop(0, 4, widen, 0)


def spread(table, level, side, rows):
    return jnp.concatenate(
        [jnp.broadcast_to(table[level, side, pl.ds(r, 1), :], (8, 128)) for r in rows], axis=0
    )


def halves(value):
    high = value.astype(BF16)
    low = (value - high.astype(F32)).astype(BF16)
    return high, low


def merge(level, tiles, js, cos_ref, sin_ref, basis_ref):
    place = merge_place(level)
    count = len(js)
    low = 1 << place
    if level % 2 == 0:
        starts = [i for i in range(16) if not i & low]
        pairs = [((k, i), (k, i + low)) for k in range(count) for i in starts]
        rows = [[js[k] * 16 + 8 * c + p for k in range(count) for p in range(8)] for c in range(2)]
    else:
        apart = low * count // 16
        firsts = [k for k in range(count) if not k & apart]
        pairs = [((k, i), (k + apart, i)) for k in firsts for i in range(16)]
        rows = [[js[k + c * apart] * 16 + i for k in firsts for i in range(16)] for c in range(2)]
    lower = jnp.concatenate([tiles[p] for p, _ in pairs], axis=0)
    upper = jnp.concatenate([tiles[q] for _, q in pairs], axis=0)
    lower_r = pltpu.roll(lower, 64, 1)
    upper_r = pltpu.roll(upper, 64, 1)
    high, rest = [], []
    for kid in rows:
        down = lower * spread(cos_ref, level, 0, kid) + lower_r * spread(sin_ref, level, 0, kid)
        up = upper * spread(cos_ref, level, 1, kid) + upper_r * spread(sin_ref, level, 1, kid)
        (down_h, down_r), (up_h, up_r) = halves(down), halves(up)
        high.append(jnp.concatenate([down_h, up_h], axis=1))
        rest.append(jnp.concatenate([down_r, up_r], axis=1))
    weights = basis_ref[level % 2]
    both = jnp.dot(jnp.concatenate(high, axis=0), weights, preferred_element_type=F32)
    both = both + jnp.dot(jnp.concatenate(rest, axis=0), weights, preferred_element_type=F32)
    result = both[:, :128] + both[:, 128:]
    after = [p for p, _ in pairs] + [q for _, q in pairs]
    return {at: result[8 * n : 8 * n + 8] for n, at in enumerate(after)}


def send_order():
    def hops(a, b):
        steps = (a // 2, a % 2 + 2 * (b // 8), b // 2 % 4)
        return sum(min(step, 4 - step) for step in steps)

    order = []
    for start in (0, 2, 1, 3):
        parts = (start, start + 8, start + 4, start + 12)
        quarter = [((3 * i + 5 * u) % 8, b) for i in range(8) for u, b in enumerate(parts)]
        order += sorted(quarter, key=lambda to: -hops(*to))
    return [to for to in order if to != (0, 0)]


def kernel(speed_hbm, offset_hbm, wide, out_ref, speed_ref, offset_ref,
           data, cos_ref, sin_ref, basis_ref, load_sem, send_sem, recv_sem):
    src, tgt = lax.axis_index("src"), lax.axis_index("tgt")
    me = src * 16 + tgt
    n = 128

    def peer(a, b):
        return lax.rem(src + a, 8), lax.rem(tgt + b, 16)

    loads = [
        pltpu.make_async_copy(speed_hbm, speed_ref, load_sem.at[0]),
        pltpu.make_async_copy(offset_hbm, offset_ref, load_sem.at[1]),
    ]
    for load in loads:
        load.start()
    barrier = pltpu.get_barrier_semaphore()
    for a in range(8):
        for b in range(16):
            if a or b:
                pl.semaphore_signal(barrier, inc=1, device_id=peer(a, b), device_id_type=MESH)
    for load in loads:
        load.wait()

    entry = 4 * (src // 2) + 5 * (src % 2 + 2 * (tgt // 8)) + 8 * (tgt // 2 % 4)
    ahead = lax.div(AHEAD - entry, 6)

    group = me * 8 // 32
    anchor = [offset_ref[c, group] for c in range(4)]
    speed = [speed_ref[a, b] for a in range(2) for b in range(3)]

    def table(level, wanted):
        @pl.when(wanted)
        def _():
            make_tables(level, speed, anchor, cos_ref, sin_ref)

    for level in range(9):
        table(level, level < ahead)
    pl.semaphore_wait(barrier, n - 1)

    def columns(owner):
        return wide.at[:, pl.ds(pl.multiple_of(owner * 8, 8), 8), :]

    pltpu.make_async_copy(columns(me), data.at[tgt, src], recv_sem.at[0]).start()

    def send(a, b):
        to = peer(a, b)
        pltpu.make_async_remote_copy(
            src_ref=columns(to[0] * 16 + to[1]),
            dst_ref=data.at[tgt, src],
            send_sem=send_sem,
            recv_sem=recv_sem.at[b],
            device_id=to,
            device_id_type=MESH,
        ).start()

    for a, b in send_order():
        send(a, b)
    for level in range(9):
        table(level, level >= ahead)
    for axis in range(2):
        make_basis(axis, basis_ref)

    boxes = data.reshape(16, 16, 8, 128)
    tables = (cos_ref, sin_ref, basis_ref)

    def quarter(q, carry):
        b = lax.rem(q, 2) * 2 + q // 2
        for part in (b, b + 8, b + 4, b + 12):
            here = data.at[lax.rem(tgt - part + 16, 16)]
            pltpu.make_async_copy(here, here, recv_sem.at[part]).wait()
        j0 = lax.rem(tgt - b + 16, 4)
        js = [j0 + 4 * k for k in range(4)]
        tiles = {(k, i): boxes[js[k], i] for k in range(4) for i in range(16)}
        for level in range(5):
            tiles = merge(level, tiles, js, *tables)
        for (k, i), value in tiles.items():
            boxes[js[k], i] = value
        return carry

    def half(b, carry):
        lax.fori_loop(2 * b, 2 * b + 2, quarter, 0)
        j0 = lax.rem(tgt - b + 16, 2)
        js = [j0 + 2 * k for k in range(8)]
        tiles = {(k, i): boxes[js[k], i] for k in range(8) for i in range(16)}
        for level in (5, 6):
            tiles = merge(level, tiles, js, *tables)
        for (k, i), value in tiles.items():
            boxes[js[k], i] = value
        return carry

    lax.fori_loop(0, 2, half, 0)
    js = list(range(16))
    tiles = {(k, i): boxes[k, i] for k in js for i in range(16)}
    tiles = merge(7, tiles, js, *tables)
    for k in js:
        block = jnp.concatenate([tiles[k, i] for i in range(16)], axis=0)
        rows = [k * 16 + i for i in range(16)]
        block = block * spread(cos_ref, 8, 0, rows) + pltpu.roll(block, 64, 1) * spread(
            sin_ref, 8, 0, rows
        )
        for i in range(16):
            out_ref[i, k] = block[8 * i : 8 * i + 8]
    sent = data.reshape(128, 2, 8, 128).at[pl.ds(0, n - 1)]
    pltpu.make_async_copy(sent, sent, send_sem).wait()


def on_device(source_weights, wave_speed, offsets):
    vmem = pl.BlockSpec(memory_space=pltpu.VMEM)
    anywhere = pl.BlockSpec(memory_space=pltpu.HBM)
    return pl.pallas_call(
        kernel,
        out_shape=jax.ShapeDtypeStruct((16, 16, 8, 128), F32),
        in_specs=[anywhere, anywhere, vmem],
        out_specs=vmem,
        scratch_shapes=[
            pltpu.SMEM((2, 3), F32),
            pltpu.SMEM((4, 32), F32),
            pltpu.VMEM((16, 8, 2, 8, 128), F32),
            pltpu.VMEM((9, 2, 256, 128), F32),
            pltpu.VMEM((9, 2, 256, 128), F32),
            pltpu.VMEM((2, 256, 256), BF16),
            pltpu.SemaphoreType.DMA((2,)),
            pltpu.SemaphoreType.DMA,
            pltpu.SemaphoreType.DMA((16,)),
        ],
        compiler_params=pltpu.CompilerParams(
            collective_id=0, has_side_effects=True, vmem_limit_bytes=VMEM_BYTES
        ),
    )(wave_speed, offsets.T, source_weights.astype(F32).reshape(2, 1024, 128))


def solution(mesh):
    in_specs = (P("src", "tgt", None, None), P(), P())
    out_specs = P(None, None, ("src", "tgt"), None)
    return jax.shard_map(
        on_device, mesh=mesh, in_specs=in_specs, out_specs=out_specs, check_vma=False
    )
```

```python
import functools
import math

import jax
import jax.numpy as jnp
import numpy as np
from jax import lax
from jax.experimental import pallas as pl
from jax.experimental.pallas import tpu as pltpu
from jax.sharding import PartitionSpec as P

POINTS = 8
HALF_SCALE = 2048.0
VMEM_BYTES = 48 << 20
AHEAD = 56
MESH = pl.DeviceIdType.MESH
F32 = jnp.float32
BF16 = jnp.bfloat16


def node_values():
    return [float(v) for v in 0.5 - 0.5 * np.cos((2.0 * np.arange(8) + 1.0) * (math.pi / 16.0))]


def pick(index, values):
    result = jnp.full(index.shape, values[0], F32)
    for at in range(1, len(values)):
        result = jnp.where(index == at, values[at], result)
    return result


def make_basis(axis, basis_ref):
    z = node_values()
    gaps = [math.prod(z[t] - z[a] for a in range(8) if a != t) for t in range(8)]
    col = lax.broadcasted_iota(jnp.int32, (16, 128), 1)

    def step(k, carry):
        row = lax.broadcasted_iota(jnp.int32, (16, 128), 0) + k * 16
        row_points, col_points = ((row >> 3) & 7, row & 7), ((col >> 3) & 7, col & 7)
        t = col_points[axis]
        u = ((row >> 7).astype(F32) + pick(row_points[axis], z)) * 0.5
        value = 1.0 / pick(t, gaps)
        for at in range(8):
            value = value * jnp.where(t == at, 1.0, u - z[at])
        same = (row_points[1 - axis] == col_points[1 - axis]) & (((row >> 6) & 1) == (col >> 6))
        high, low = halves(jnp.where(same, value, 0.0))
        rows = pl.ds(pl.multiple_of(k * 16, 16), 16)
        basis_ref[axis, rows, 0:128] = high
        basis_ref[axis, rows, 128:256] = low
        return carry

    lax.fori_loop(0, 16, step, 0)


def displacement(level, which):
    z = node_values()
    lane = lax.broadcasted_iota(jnp.int32, (8, 128), 1)
    dim = which % 2
    width = 2.0 ** ((level // 2 + 1, (level + 1) // 2)[dim] - 10)
    point = pick((lane & 7) if dim else ((lane >> 3) & 7), z)
    if which < 2 and level % 2 == dim:
        return (point + (lane >> 6).astype(F32)) * (width / 2)
    return point * width


def sine_cosine(half):
    turns = half * (1.0 / math.pi) + 12582912.0
    turns = turns - 12582912.0
    rest = half - turns * 3.140625
    rest = rest - turns * 9.67653589793e-4
    sq = rest * rest
    sine = ((5.1995018e-6 * sq - 3.9612958e-4) * sq + 1.66660308e-2) * sq - 3.3333314e-1
    sine = (sine * sq + 2.0) * rest
    cosine = (2.337661e-5 * sq - 1.3865138e-3) * sq + 4.1665433e-2
    cosine = (cosine * sq - 0.5) * sq + 1.0
    return sine * cosine, 1.0 - 0.5 * (sine * sine)


def source_index(box, done):
    total = box * 0
    for place in range(4 - done):
        total = total + (((box >> place) & 1) << (3 - done - place))
    return total


def part_of(box, done, target_anchor, source_anchor, slopes, shifts, delta):
    x = target_anchor + ((box >> (4 - done)).astype(F32) + 0.5) * (2.0 ** (-2 - done))
    r = source_anchor + source_index(box, done).astype(F32) * (2.0 ** (done - 10))
    first, second = slopes[0] * x, slopes[1] * x
    if shifts is not None:
        first, second = shifts[0] + first, shifts[1] + second
    k = r + delta
    scaled = delta * HALF_SCALE
    return first, second, scaled * (k + r), k * k, r * r, x * scaled


def half_angle(one, two):
    s1, s2 = one[0] + two[0], one[1] + two[1]
    a1, a2 = s1 * s1, s2 * s2
    over = a1 * one[2] + a2 * two[2]
    there = a1 * one[3] + a2 * two[3]
    here = a1 * one[4] + a2 * two[4]
    under = there * lax.rsqrt(there) + here * lax.rsqrt(here)
    return (one[5] + two[5]) + over / under


def merge_place(level):
    return 3 - level // 2


def make_tables(level, speed, anchor, cos_ref, sin_ref):
    lane = lax.broadcasted_iota(jnp.int32, (8, 128), 1)
    row = lax.broadcasted_iota(jnp.int32, (8, 128), 0)
    upper = lane >= 64
    side = jnp.where(upper, 1, 0)
    place = merge_place(level)
    low = (1 << place) - 1 if level < 8 else 0

    def first(box, at, which):
        return part_of(
            box, at // 2 + 1, anchor[0], anchor[2], (speed[1], speed[4]), (speed[0], speed[3]),
            displacement(at, which),
        )

    def second(box, at, which):
        return part_of(
            box, (at + 1) // 2, anchor[1], anchor[3], (speed[2], speed[5]), None,
            displacement(at, which),
        )

    def store(angle, at):
        sine, cosine = sine_cosine(angle)
        rows = pl.ds(pl.multiple_of(at, 8), 8)
        cos_ref[level, 0, rows, :] = cosine
        sin_ref[level, 0, rows, :] = sine if level < 8 else jnp.where(upper, sine, -sine)

    if level == 8:
        ones = [first(row + 8 * half, 7, 2) for half in range(2)]

        def step(jj, carry):
            for j in (2 * jj, 2 * jj + 1):
                two = second(j, 7, 3)
                for half in range(2):
                    store(-half_angle(ones[half], two), j * 16 + 8 * half)
            return carry

    elif level % 2 == 0:
        pair = ((row & ~low) << 1) | (row & low)
        ones = [first(pair | (c << place), level, 0) for c in range(2)]
        if level > 0:
            outs = first(pair | (side << place), level - 1, 2)

        def step(jj, carry):
            for j in (2 * jj, 2 * jj + 1):
                two = second(j, level, 1)
                if level > 0:
                    out = half_angle(outs, second(j, level - 1, 3))
                for c in range(2):
                    angle = half_angle(ones[c], two)
                    if level > 0:
                        angle = angle - out
                    store(angle, j * 16 + 8 * c)
            return carry

    else:
        ones = [first(row + 8 * half, level, 0) for half in range(2)]
        outs = [first(row + 8 * half, level - 1, 2) for half in range(2)]

        def step(jj, carry):
            j0 = ((jj >> place) << (place + 1)) | (jj & low)
            two_out = second(j0 + (side << place), level - 1, 3)
            out = [half_angle(outs[half], two_out) for half in range(2)]
            for c in range(2):
                j = j0 + (c << place)
                two = second(j, level, 1)
                for half in range(2):
                    store(half_angle(ones[half], two) - out[half], j * 16 + 8 * half)
            return carry

    lax.fori_loop(0, 8, step, 0)
    if level == 8:
        return

    def widen(k, carry):
        rows = [pl.ds(pl.multiple_of(k * 64 + 8 * q, 8), 8) for q in range(8)]
        sines = [sin_ref[level, 0, r, :] for r in rows]
        cosines = [cos_ref[level, 0, r, :] for r in rows]
        sines_r = [pltpu.roll(v, 64, 1) for v in sines]
        cosines_r = [pltpu.roll(v, 64, 1) for v in cosines]
        for r, sine, cosine, sine_r, cosine_r in zip(rows, sines, cosines, sines_r, cosines_r):
            cos_ref[level, 0, r, :] = jnp.where(upper, cosine_r, cosine)
            cos_ref[level, 1, r, :] = jnp.where(upper, cosine, cosine_r)
            sin_ref[level, 0, r, :] = jnp.where(upper, sine_r, -sine)
            sin_ref[level, 1, r, :] = jnp.where(upper, sine, -sine_r)
        return carry

    lax.fori_loop(0, 4, widen, 0)


def spread(table, level, side, rows):
    return jnp.concatenate(
        [jnp.broadcast_to(table[level, side, pl.ds(r, 1), :], (8, 128)) for r in rows], axis=0
    )


def halves(value):
    high = value.astype(BF16)
    low = (value - high.astype(F32)).astype(BF16)
    return high, low


def merge(level, tiles, js, cos_ref, sin_ref, basis_ref):
    place = merge_place(level)
    count = len(js)
    low = 1 << place
    if level % 2 == 0:
        starts = [i for i in range(16) if not i & low]
        pairs = [((k, i), (k, i + low)) for k in range(count) for i in starts]
        rows = [[js[k] * 16 + 8 * c + p for k in range(count) for p in range(8)] for c in range(2)]
    else:
        apart = low * count // 16
        firsts = [k for k in range(count) if not k & apart]
        pairs = [((k, i), (k + apart, i)) for k in firsts for i in range(16)]
        rows = [[js[k + c * apart] * 16 + i for k in firsts for i in range(16)] for c in range(2)]
    lower = jnp.concatenate([tiles[p] for p, _ in pairs], axis=0)
    upper = jnp.concatenate([tiles[q] for _, q in pairs], axis=0)
    lower_r = pltpu.roll(lower, 64, 1)
    upper_r = pltpu.roll(upper, 64, 1)
    high, rest = [], []
    for kid in rows:
        down = lower * spread(cos_ref, level, 0, kid) + lower_r * spread(sin_ref, level, 0, kid)
        up = upper * spread(cos_ref, level, 1, kid) + upper_r * spread(sin_ref, level, 1, kid)
        (down_h, down_r), (up_h, up_r) = halves(down), halves(up)
        high.append(jnp.concatenate([down_h, up_h], axis=1))
        rest.append(jnp.concatenate([down_r, up_r], axis=1))
    weights = basis_ref[level % 2]
    twice = jnp.concatenate([weights, weights], axis=0)
    result = []
    for h, r in zip(high, rest):
        both = jnp.dot(jnp.concatenate([h, r], axis=1), twice, preferred_element_type=F32)
        result.append(both[:, :128] + both[:, 128:])
    result = jnp.concatenate(result, axis=0)
    after = [p for p, _ in pairs] + [q for _, q in pairs]
    return {at: result[8 * n : 8 * n + 8] for n, at in enumerate(after)}


def send_order():
    def hops(a, b):
        steps = (a // 2, a % 2 + 2 * (b // 8), b // 2 % 4)
        return sum(min(step, 4 - step) for step in steps)

    order = []
    for start in (0, 2, 1, 3):
        parts = (start, start + 8, start + 4, start + 12)
        quarter = [((3 * i + 5 * u) % 8, b) for i in range(8) for u, b in enumerate(parts)]
        order += sorted(quarter, key=lambda to: -hops(*to))
    return [to for to in order if to != (0, 0)]


def kernel(speed_hbm, offset_hbm, wide, out_ref, speed_ref, offset_ref,
           data, cos_ref, sin_ref, basis_ref, load_sem, send_sem, recv_sem):
    src, tgt = lax.axis_index("src"), lax.axis_index("tgt")
    me = src * 16 + tgt
    n = 128

    def peer(a, b):
        return lax.rem(src + a, 8), lax.rem(tgt + b, 16)

    loads = [
        pltpu.make_async_copy(speed_hbm, speed_ref, load_sem.at[0]),
        pltpu.make_async_copy(offset_hbm, offset_ref, load_sem.at[1]),
    ]
    for load in loads:
        load.start()
    barrier = pltpu.get_barrier_semaphore()
    for a in range(8):
        for b in range(16):
            if a or b:
                pl.semaphore_signal(barrier, inc=1, device_id=peer(a, b), device_id_type=MESH)
    for load in loads:
        load.wait()

    entry = 4 * (src // 2) + 5 * (src % 2 + 2 * (tgt // 8)) + 8 * (tgt // 2 % 4)
    ahead = lax.div(AHEAD - entry, 6)

    group = me * 8 // 32
    anchor = [offset_ref[c, group] for c in range(4)]
    speed = [speed_ref[a, b] for a in range(2) for b in range(3)]

    def table(level, wanted):
        @pl.when(wanted)
        def _():
            make_tables(level, speed, anchor, cos_ref, sin_ref)

    for level in range(9):
        table(level, level < ahead)
    pl.semaphore_wait(barrier, n - 1)

    def columns(owner):
        return wide.at[:, pl.ds(pl.multiple_of(owner * 8, 8), 8), :]

    pltpu.make_async_copy(columns(me), data.at[tgt, src], recv_sem.at[0]).start()

    def send(a, b):
        to = peer(a, b)
        pltpu.make_async_remote_copy(
            src_ref=columns(to[0] * 16 + to[1]),
            dst_ref=data.at[tgt, src],
            send_sem=send_sem,
            recv_sem=recv_sem.at[b],
            device_id=to,
            device_id_type=MESH,
        ).start()

    for a, b in send_order():
        send(a, b)
    for level in range(9):
        table(level, level >= ahead)
    for axis in range(2):
        make_basis(axis, basis_ref)

    boxes = data.reshape(16, 16, 8, 128)
    tables = (cos_ref, sin_ref, basis_ref)

    def quarter(q, carry):
        b = lax.rem(q, 2) * 2 + q // 2
        for part in (b, b + 8, b + 4, b + 12):
            here = data.at[lax.rem(tgt - part + 16, 16)]
            pltpu.make_async_copy(here, here, recv_sem.at[part]).wait()
        j0 = lax.rem(tgt - b + 16, 4)
        js = [j0 + 4 * k for k in range(4)]
        tiles = {(k, i): boxes[js[k], i] for k in range(4) for i in range(16)}
        for level in range(5):
            tiles = merge(level, tiles, js, *tables)
        for (k, i), value in tiles.items():
            boxes[js[k], i] = value
        return carry

    def half(b, carry):
        lax.fori_loop(2 * b, 2 * b + 2, quarter, 0)
        j0 = lax.rem(tgt - b + 16, 2)
        js = [j0 + 2 * k for k in range(8)]
        tiles = {(k, i): boxes[js[k], i] for k in range(8) for i in range(16)}
        for level in (5, 6):
            tiles = merge(level, tiles, js, *tables)
        for (k, i), value in tiles.items():
            boxes[js[k], i] = value
        return carry

    lax.fori_loop(0, 2, half, 0)
    js = list(range(16))
    tiles = {(k, i): boxes[k, i] for k in js for i in range(16)}
    tiles = merge(7, tiles, js, *tables)
    for k in js:
        block = jnp.concatenate([tiles[k, i] for i in range(16)], axis=0)
        rows = [k * 16 + i for i in range(16)]
        block = block * spread(cos_ref, 8, 0, rows) + pltpu.roll(block, 64, 1) * spread(
            sin_ref, 8, 0, rows
        )
        for i in range(16):
            out_ref[i, k] = block[8 * i : 8 * i + 8]
    sent = data.reshape(128, 2, 8, 128).at[pl.ds(0, n - 1)]
    pltpu.make_async_copy(sent, sent, send_sem).wait()


def on_device(source_weights, wave_speed, offsets):
    vmem = pl.BlockSpec(memory_space=pltpu.VMEM)
    anywhere = pl.BlockSpec(memory_space=pltpu.HBM)
    return pl.pallas_call(
        kernel,
        out_shape=jax.ShapeDtypeStruct((16, 16, 8, 128), F32),
        in_specs=[anywhere, anywhere, vmem],
        out_specs=vmem,
        scratch_shapes=[
            pltpu.SMEM((2, 3), F32),
            pltpu.SMEM((4, 32), F32),
            pltpu.VMEM((16, 8, 2, 8, 128), F32),
            pltpu.VMEM((9, 2, 256, 128), F32),
            pltpu.VMEM((9, 2, 256, 128), F32),
            pltpu.VMEM((2, 256, 256), BF16),
            pltpu.SemaphoreType.DMA((2,)),
            pltpu.SemaphoreType.DMA,
            pltpu.SemaphoreType.DMA((16,)),
        ],
        compiler_params=pltpu.CompilerParams(
            collective_id=0, has_side_effects=True, vmem_limit_bytes=VMEM_BYTES
        ),
    )(wave_speed, offsets.T, source_weights.astype(F32).reshape(2, 1024, 128))


def solution(mesh):
    in_specs = (P("src", "tgt", None, None), P(), P())
    out_specs = P(None, None, ("src", "tgt"), None)
    return jax.shard_map(
        on_device, mesh=mesh, in_specs=in_specs, out_specs=out_specs, check_vma=False
    )
```

```python
import functools
import math

import jax
import jax.numpy as jnp
import numpy as np
from jax import lax
from jax.experimental import pallas as pl
from jax.experimental.pallas import tpu as pltpu
from jax.sharding import PartitionSpec as P

POINTS = 8
HALF_SCALE = 2048.0
VMEM_BYTES = 48 << 20
AHEAD = 56
MESH = pl.DeviceIdType.MESH
F32 = jnp.float32
BF16 = jnp.bfloat16


def node_values():
    return [float(v) for v in 0.5 - 0.5 * np.cos((2.0 * np.arange(8) + 1.0) * (math.pi / 16.0))]


def pick(index, values):
    result = jnp.full(index.shape, values[0], F32)
    for at in range(1, len(values)):
        result = jnp.where(index == at, values[at], result)
    return result


def make_basis(axis, basis_ref):
    z = node_values()
    gaps = [math.prod(z[t] - z[a] for a in range(8) if a != t) for t in range(8)]
    col = lax.broadcasted_iota(jnp.int32, (16, 128), 1)

    def step(k, carry):
        row = lax.broadcasted_iota(jnp.int32, (16, 128), 0) + k * 16
        row_points, col_points = ((row >> 3) & 7, row & 7), ((col >> 3) & 7, col & 7)
        t = col_points[axis]
        u = ((row >> 7).astype(F32) + pick(row_points[axis], z)) * 0.5
        value = 1.0 / pick(t, gaps)
        for at in range(8):
            value = value * jnp.where(t == at, 1.0, u - z[at])
        same = (row_points[1 - axis] == col_points[1 - axis]) & (((row >> 6) & 1) == (col >> 6))
        high, low = halves(jnp.where(same, value, 0.0))
        rows = pl.ds(pl.multiple_of(k * 16, 16), 16)
        basis_ref[axis, rows, 0:128] = high
        basis_ref[axis, rows, 128:256] = low
        return carry

    lax.fori_loop(0, 16, step, 0)


def displacement(level, which):
    z = node_values()
    lane = lax.broadcasted_iota(jnp.int32, (8, 128), 1)
    dim = which % 2
    width = 2.0 ** ((level // 2 + 1, (level + 1) // 2)[dim] - 10)
    point = pick((lane & 7) if dim else ((lane >> 3) & 7), z)
    if which < 2 and level % 2 == dim:
        return (point + (lane >> 6).astype(F32)) * (width / 2)
    return point * width


def sine_cosine(half):
    turns = half * (1.0 / math.pi) + 12582912.0
    turns = turns - 12582912.0
    rest = half - turns * 3.140625
    rest = rest - turns * 9.67653589793e-4
    sq = rest * rest
    sine = ((5.1995018e-6 * sq - 3.9612958e-4) * sq + 1.66660308e-2) * sq - 3.3333314e-1
    sine = (sine * sq + 2.0) * rest
    cosine = (2.337661e-5 * sq - 1.3865138e-3) * sq + 4.1665433e-2
    cosine = (cosine * sq - 0.5) * sq + 1.0
    return sine * cosine, 1.0 - 0.5 * (sine * sine)


def source_index(box, done):
    total = box * 0
    for place in range(4 - done):
        total = total + (((box >> place) & 1) << (3 - done - place))
    return total


def part_of(box, done, target_anchor, source_anchor, slopes, shifts, delta):
    x = target_anchor + ((box >> (4 - done)).astype(F32) + 0.5) * (2.0 ** (-2 - done))
    r = source_anchor + source_index(box, done).astype(F32) * (2.0 ** (done - 10))
    first, second = slopes[0] * x, slopes[1] * x
    if shifts is not None:
        first, second = shifts[0] + first, shifts[1] + second
    k = r + delta
    scaled = delta * HALF_SCALE
    return first, second, scaled * (k + r), k * k, r * r, x * scaled


def half_angle(one, two):
    s1, s2 = one[0] + two[0], one[1] + two[1]
    a1, a2 = s1 * s1, s2 * s2
    over = a1 * one[2] + a2 * two[2]
    there = a1 * one[3] + a2 * two[3]
    here = a1 * one[4] + a2 * two[4]
    under = there * lax.rsqrt(there) + here * lax.rsqrt(here)
    return (one[5] + two[5]) + over / under


def merge_place(level):
    return 3 - level // 2


def make_tables(level, speed, anchor, cos_ref, sin_ref):
    lane = lax.broadcasted_iota(jnp.int32, (8, 128), 1)
    row = lax.broadcasted_iota(jnp.int32, (8, 128), 0)
    upper = lane >= 64
    side = jnp.where(upper, 1, 0)
    place = merge_place(level)
    low = (1 << place) - 1 if level < 8 else 0

    def first(box, at, which):
        return part_of(
            box, at // 2 + 1, anchor[0], anchor[2], (speed[1], speed[4]), (speed[0], speed[3]),
            displacement(at, which),
        )

    def second(box, at, which):
        return part_of(
            box, (at + 1) // 2, anchor[1], anchor[3], (speed[2], speed[5]), None,
            displacement(at, which),
        )

    def store(angle, at):
        sine, cosine = sine_cosine(angle)
        rows = pl.ds(pl.multiple_of(at, 8), 8)
        cos_ref[level, 0, rows, :] = cosine
        sin_ref[level, 0, rows, :] = sine if level < 8 else jnp.where(upper, sine, -sine)

    if level == 8:
        ones = [first(row + 8 * half, 7, 2) for half in range(2)]

        def step(jj, carry):
            for j in (2 * jj, 2 * jj + 1):
                two = second(j, 7, 3)
                for half in range(2):
                    store(-half_angle(ones[half], two), j * 16 + 8 * half)
            return carry

    elif level % 2 == 0:
        pair = ((row & ~low) << 1) | (row & low)
        ones = [first(pair | (c << place), level, 0) for c in range(2)]
        if level > 0:
            outs = first(pair | (side << place), level - 1, 2)

        def step(jj, carry):
            for j in (2 * jj, 2 * jj + 1):
                two = second(j, level, 1)
                if level > 0:
                    out = half_angle(outs, second(j, level - 1, 3))
                for c in range(2):
                    angle = half_angle(ones[c], two)
                    if level > 0:
                        angle = angle - out
                    store(angle, j * 16 + 8 * c)
            return carry

    else:
        ones = [first(row + 8 * half, level, 0) for half in range(2)]
        outs = [first(row + 8 * half, level - 1, 2) for half in range(2)]

        def step(jj, carry):
            j0 = ((jj >> place) << (place + 1)) | (jj & low)
            two_out = second(j0 + (side << place), level - 1, 3)
            out = [half_angle(outs[half], two_out) for half in range(2)]
            for c in range(2):
                j = j0 + (c << place)
                two = second(j, level, 1)
                for half in range(2):
                    store(half_angle(ones[half], two) - out[half], j * 16 + 8 * half)
            return carry

    lax.fori_loop(0, 8, step, 0)
    if level == 8:
        return

    def widen(k, carry):
        rows = [pl.ds(pl.multiple_of(k * 64 + 8 * q, 8), 8) for q in range(8)]
        sines = [sin_ref[level, 0, r, :] for r in rows]
        cosines = [cos_ref[level, 0, r, :] for r in rows]
        sines_r = [pltpu.roll(v, 64, 1) for v in sines]
        cosines_r = [pltpu.roll(v, 64, 1) for v in cosines]
        for r, sine, cosine, sine_r, cosine_r in zip(rows, sines, cosines, sines_r, cosines_r):
            cos_ref[level, 0, r, :] = jnp.where(upper, cosine_r, cosine)
            cos_ref[level, 1, r, :] = jnp.where(upper, cosine, cosine_r)
            sin_ref[level, 0, r, :] = jnp.where(upper, sine_r, -sine)
            sin_ref[level, 1, r, :] = jnp.where(upper, sine, -sine_r)
        return carry

    lax.fori_loop(0, 4, widen, 0)


def spread(table, level, side, rows):
    return jnp.concatenate(
        [jnp.broadcast_to(table[level, side, pl.ds(r, 1), :], (8, 128)) for r in rows], axis=0
    )


def halves(value):
    high = value.astype(BF16)
    low = (value - high.astype(F32)).astype(BF16)
    return high, low


def merge(level, tiles, js, cos_ref, sin_ref, basis_ref):
    place = merge_place(level)
    count = len(js)
    low = 1 << place
    if level % 2 == 0:
        starts = [i for i in range(16) if not i & low]
        pairs = [((k, i), (k, i + low)) for k in range(count) for i in starts]
        rows = [[js[k] * 16 + 8 * c + p for k in range(count) for p in range(8)] for c in range(2)]
    else:
        apart = low * count // 16
        firsts = [k for k in range(count) if not k & apart]
        pairs = [((k, i), (k + apart, i)) for k in firsts for i in range(16)]
        rows = [[js[k + c * apart] * 16 + i for k in firsts for i in range(16)] for c in range(2)]
    lower = jnp.concatenate([tiles[p] for p, _ in pairs], axis=0)
    upper = jnp.concatenate([tiles[q] for _, q in pairs], axis=0)
    lower_r = pltpu.roll(lower, 64, 1)
    upper_r = pltpu.roll(upper, 64, 1)
    high, rest = [], []
    for kid in rows:
        down = lower * spread(cos_ref, level, 0, kid) + lower_r * spread(sin_ref, level, 0, kid)
        up = upper * spread(cos_ref, level, 1, kid) + upper_r * spread(sin_ref, level, 1, kid)
        (down_h, down_r), (up_h, up_r) = halves(down), halves(up)
        high.append(jnp.concatenate([down_h, up_h], axis=1))
        rest.append(jnp.concatenate([down_r, up_r], axis=1))
    weights = basis_ref[level % 2]
    twice = jnp.concatenate([weights, weights], axis=0)
    result = []
    for h, r in zip(high, rest):
        both = jnp.dot(jnp.concatenate([h, r], axis=1), twice, preferred_element_type=F32)
        result.append(both[:, :128] + both[:, 128:])
    result = jnp.concatenate(result, axis=0)
    after = [p for p, _ in pairs] + [q for _, q in pairs]
    return {at: result[8 * n : 8 * n + 8] for n, at in enumerate(after)}


def send_order():
    def hops(a, b):
        steps = (a // 2, a % 2 + 2 * (b // 8), b // 2 % 4)
        return sum(min(step, 4 - step) for step in steps)

    order = []
    for start in (0, 2, 1, 3):
        parts = (start, start + 8, start + 4, start + 12)
        quarter = [((i + 2 * u) % 8, b) for i in range(8) for u, b in enumerate(parts)]
        order += sorted(quarter, key=lambda to: -hops(*to))
    return [to for to in order if to != (0, 0)]


def kernel(speed_hbm, offset_hbm, wide, out_ref, speed_ref, offset_ref,
           data, cos_ref, sin_ref, basis_ref, load_sem, send_sem, recv_sem):
    src, tgt = lax.axis_index("src"), lax.axis_index("tgt")
    me = src * 16 + tgt
    n = 128

    def peer(a, b):
        return lax.rem(src + a, 8), lax.rem(tgt + b, 16)

    loads = [
        pltpu.make_async_copy(speed_hbm, speed_ref, load_sem.at[0]),
        pltpu.make_async_copy(offset_hbm, offset_ref, load_sem.at[1]),
    ]
    for load in loads:
        load.start()
    barrier = pltpu.get_barrier_semaphore()
    for a in range(8):
        for b in range(16):
            if a or b:
                pl.semaphore_signal(barrier, inc=1, device_id=peer(a, b), device_id_type=MESH)
    for load in loads:
        load.wait()

    entry = 4 * (src // 2) + 5 * (src % 2 + 2 * (tgt // 8)) + 8 * (tgt // 2 % 4)
    ahead = lax.div(AHEAD - entry, 6)

    group = me * 8 // 32
    anchor = [offset_ref[c, group] for c in range(4)]
    speed = [speed_ref[a, b] for a in range(2) for b in range(3)]

    def table(level, wanted):
        @pl.when(wanted)
        def _():
            make_tables(level, speed, anchor, cos_ref, sin_ref)

    for level in range(9):
        table(level, level < ahead)
    pl.semaphore_wait(barrier, n - 1)

    def columns(owner):
        return wide.at[owner]

    pltpu.make_async_copy(columns(me), data.at[tgt, src], recv_sem.at[0]).start()

    def send(a, b):
        to = peer(a, b)
        pltpu.make_async_remote_copy(
            src_ref=columns(to[0] * 16 + to[1]),
            dst_ref=data.at[tgt, src],
            send_sem=send_sem,
            recv_sem=recv_sem.at[b],
            device_id=to,
            device_id_type=MESH,
        ).start()

    for a, b in send_order():
        send(a, b)
    for level in range(9):
        table(level, level >= ahead)
    for axis in range(2):
        make_basis(axis, basis_ref)

    boxes = data.reshape(16, 16, 8, 128)
    tables = (cos_ref, sin_ref, basis_ref)

    def quarter(q, carry):
        b = lax.rem(q, 2) * 2 + q // 2
        for part in (b, b + 8, b + 4, b + 12):
            here = data.at[lax.rem(tgt - part + 16, 16)]
            pltpu.make_async_copy(here, here, recv_sem.at[part]).wait()
        j0 = lax.rem(tgt - b + 16, 4)
        js = [j0 + 4 * k for k in range(4)]
        tiles = {(k, i): boxes[js[k], i] for k in range(4) for i in range(16)}
        for level in range(5):
            tiles = merge(level, tiles, js, *tables)
        for (k, i), value in tiles.items():
            boxes[js[k], i] = value
        return carry

    def half(b, carry):
        lax.fori_loop(2 * b, 2 * b + 2, quarter, 0)
        j0 = lax.rem(tgt - b + 16, 2)
        js = [j0 + 2 * k for k in range(8)]
        tiles = {(k, i): boxes[js[k], i] for k in range(8) for i in range(16)}
        for level in (5, 6):
            tiles = merge(level, tiles, js, *tables)
        for (k, i), value in tiles.items():
            boxes[js[k], i] = value
        return carry

    lax.fori_loop(0, 2, half, 0)
    js = list(range(16))
    tiles = {(k, i): boxes[k, i] for k in js for i in range(16)}
    tiles = merge(7, tiles, js, *tables)
    for k in js:
        block = jnp.concatenate([tiles[k, i] for i in range(16)], axis=0)
        rows = [k * 16 + i for i in range(16)]
        block = block * spread(cos_ref, 8, 0, rows) + pltpu.roll(block, 64, 1) * spread(
            sin_ref, 8, 0, rows
        )
        for i in range(16):
            out_ref[i, k] = block[8 * i : 8 * i + 8]
    sent = data.reshape(128, 2, 8, 128).at[pl.ds(0, n - 1)]
    pltpu.make_async_copy(sent, sent, send_sem).wait()


def on_device(source_weights, wave_speed, offsets):
    vmem = pl.BlockSpec(memory_space=pltpu.VMEM)
    anywhere = pl.BlockSpec(memory_space=pltpu.HBM)
    return pl.pallas_call(
        kernel,
        out_shape=jax.ShapeDtypeStruct((16, 16, 8, 128), F32),
        in_specs=[anywhere, anywhere, vmem],
        out_specs=vmem,
        scratch_shapes=[
            pltpu.SMEM((2, 3), F32),
            pltpu.SMEM((4, 32), F32),
            pltpu.VMEM((16, 8, 2, 8, 128), F32),
            pltpu.VMEM((9, 2, 256, 128), F32),
            pltpu.VMEM((9, 2, 256, 128), F32),
            pltpu.VMEM((2, 256, 256), BF16),
            pltpu.SemaphoreType.DMA((2,)),
            pltpu.SemaphoreType.DMA,
            pltpu.SemaphoreType.DMA((16,)),
        ],
        compiler_params=pltpu.CompilerParams(
            collective_id=0, has_side_effects=True, vmem_limit_bytes=VMEM_BYTES
        ),
    )(wave_speed, offsets.T, source_weights.astype(F32).reshape(2, 128, 8, 128).transpose(1, 0, 2, 3))


def solution(mesh):
    in_specs = (P("src", "tgt", None, None), P(), P())
    out_specs = P(None, None, ("src", "tgt"), None)
    return jax.shard_map(
        on_device, mesh=mesh, in_specs=in_specs, out_specs=out_specs, check_vma=False
    )
```
